128 devices in a mesh: row: 16 (over x_hi, z, core), col: 8 (over y, x_lo).
Axes of the slice: x: 4 (x_hi: 2, x_lo: 2; x = x_hi * 2 + x_lo), y: 4, z: 4, core: 2. Of those that a mesh axis runs over, the one named last changes fastest.
Arguments:
- pair_in: float32 [384, 384, 128], P('row', 'col'), may hold values from -6 to 6
- cotangent: float32 [384, 384, 128], P('row', 'col'), may hold values from -6 to 6
- outgoing_proj: bfloat16 [128, 512], replicated, may hold values from -0.5 to 0.5
- outgoing_gate: bfloat16 [128, 128], replicated, may hold values from -0.5 to 0.5
- outgoing_lift: bfloat16 [128, 128], replicated, may hold values from -0.5 to 0.5
- incoming_proj: bfloat16 [128, 512], replicated, may hold values from -0.5 to 0.5
- incoming_gate: bfloat16 [128, 128], replicated, may hold values from -0.5 to 0.5
- incoming_lift: bfloat16 [128, 128], replicated, may hold values from -0.5 to 0.5
Outputs:
- pair_result: float32 [384, 384, 128], P('row', 'col')
- pair_grad: float32 [384, 384, 128], P('row', 'col')
- dproj_outgoing: float32 [128, 512], replicated
- dgate_outgoing: float32 [128, 128], replicated
- dlift_outgoing: float32 [128, 128], replicated
- dproj_incoming: float32 [128, 512], replicated
- dgate_incoming: float32 [128, 128], replicated
- dlift_incoming: float32 [128, 128], replicated
The draws below stay inside these ranges and needn't reach their ends.
All inputs are finite; a program needn't handle non-finite values.
Results may differ from the reference program's by a relative error of at most 0.035.
Values may be sent and summed in bfloat16 or wider, within the bound.
A program may use at most 128 MiB of HBM per device.

```python
import jax
import jax.numpy as jnp
from jax import lax

C = 128
H = 128
TOKENS = 384


def levels(stream_key, dims, split, low, high):
    def one(position, parts):
        draws = jax.random.uniform(jax.random.fold_in(jax.random.fold_in(stream_key, 6), position), (parts,), jnp.float32, low / len(split), high / len(split))
        return jnp.repeat(jnp.exp(draws), dims[position] // parts).reshape((-1,) + (1,) * (len(dims) - position - 1))

    gain = one(*split[0])
    for cut in split[1:]:
        gain = gain * one(*cut)
    return gain


def scatter_about(key, shape, scale, reach, cuts=(), kind=jnp.bfloat16):
    values = scale * jax.random.normal(key, shape, jnp.float32)
    if cuts:
        values = values * levels(key, shape, cuts, -0.22, 0.18)
    return jnp.clip(values, -reach, reach).astype(kind)


def setup_inputs(seed: int = 0) -> dict:
    keys = jax.random.split(jax.random.key(seed), 9)
    pair_in = scatter_about(keys[0], (TOKENS, TOKENS, C), 1.0, 6.0, ((0, 16), (1, 8)), jnp.float32)
    cotangent = scatter_about(keys[1], (TOKENS, TOKENS, C), 1.0, 6.0, ((0, 16), (1, 8)), jnp.float32)
    outgoing_proj = scatter_about(keys[2], (C, 4 * H), C ** -0.5, 0.5)
    outgoing_gate = scatter_about(keys[3], (C, C), C ** -0.5, 0.5)
    outgoing_lift = scatter_about(keys[4], (H, C), H ** -0.5, 0.5)
    incoming_proj = scatter_about(keys[5], (C, 4 * H), C ** -0.5, 0.5)
    incoming_gate = scatter_about(keys[6], (C, C), C ** -0.5, 0.5)
    incoming_lift = scatter_about(keys[7], (H, C), H ** -0.5, 0.5)
    return {"pair_in": pair_in, "cotangent": cotangent, "outgoing_proj": outgoing_proj, "outgoing_gate": outgoing_gate, "outgoing_lift": outgoing_lift, "incoming_proj": incoming_proj, "incoming_gate": incoming_gate, "incoming_lift": incoming_lift}


EPSILON = 1e-05

def layer_norm(pair_field):
    mean_val = lax.optimization_barrier(jnp.mean(pair_field, axis=-1, keepdims=True))
    centred = pair_field - mean_val
    spread = jnp.sqrt(lax.optimization_barrier(jnp.mean(centred * centred, axis=-1, keepdims=True)) + EPSILON)
    return (centred / spread, spread)

def norm_back(grad_in, normed, spread):
    mean_grad = lax.optimization_barrier(jnp.mean(grad_in, axis=-1, keepdims=True))
    mean_mixed = lax.optimization_barrier(jnp.mean(grad_in * normed, axis=-1, keepdims=True))
    return (grad_in - mean_grad - normed * mean_mixed) / spread

def flat_dot(first, matrix):
    lead_shape = first.shape[:-1]
    result = jnp.dot(first.reshape(-1, first.shape[-1]), matrix, preferred_element_type=jnp.float32)
    return result.reshape(lead_shape + (matrix.shape[-1],))

def cell_sum(first, second):
    return jnp.dot(first.reshape(-1, first.shape[-1]).T, second.reshape(-1, second.shape[-1]), preferred_element_type=jnp.float32)

def project_tile(pair_field, w_proj, w_gate):
    normed, spread = layer_norm(pair_field)
    normed_b = normed.astype(jnp.bfloat16)
    pre_act = flat_dot(normed_b, w_proj)
    hidden_size = pre_act.shape[-1] // 4
    left_proj = (jax.nn.sigmoid(pre_act[..., :hidden_size]) * pre_act[..., hidden_size:2 * hidden_size]).astype(jnp.bfloat16)
    right_proj = (jax.nn.sigmoid(pre_act[..., 2 * hidden_size:3 * hidden_size]) * pre_act[..., 3 * hidden_size:]).astype(jnp.bfloat16)
    gate_val = jax.nn.sigmoid(flat_dot(normed_b, w_gate))
    return (normed, spread, normed_b, pre_act, left_proj, right_proj, gate_val)

def finish_tile(tri_sum, gate_val, w_lift):
    unit, unit_spread = layer_norm(tri_sum)
    unit_b = unit.astype(jnp.bfloat16)
    lifted = flat_dot(unit_b, w_lift)
    return (gate_val * lifted, unit, unit_spread, unit_b, lifted)

def head_back(grad_out, gate_val, lifted, unit, unit_spread, unit_b, w_lift):
    grad_lift = (grad_out * gate_val).astype(jnp.bfloat16)
    grad_gate = (grad_out * lifted * gate_val * (1.0 - gate_val)).astype(jnp.bfloat16)
    grad_unit = flat_dot(grad_lift, w_lift.T)
    dlift = cell_sum(unit_b, grad_lift)
    grad_tri = norm_back(grad_unit, unit, unit_spread).astype(jnp.bfloat16)
    return (grad_tri, grad_gate, dlift)

def tail_back(grad_out, grad_gate, grad_left, grad_right, normed, spread, normed_b, pre_act, w_proj, w_gate):
    hidden_size = pre_act.shape[-1] // 4
    sig_left = jax.nn.sigmoid(pre_act[..., :hidden_size])
    sig_right = jax.nn.sigmoid(pre_act[..., 2 * hidden_size:3 * hidden_size])
    grad_pre = jnp.concatenate([grad_left * pre_act[..., hidden_size:2 * hidden_size] * sig_left * (1.0 - sig_left), grad_left * sig_left, grad_right * pre_act[..., 3 * hidden_size:] * sig_right * (1.0 - sig_right), grad_right * sig_right], axis=-1).astype(jnp.bfloat16)
    grad_normed = flat_dot(grad_pre, w_proj.T) + flat_dot(grad_gate, w_gate.T)
    grad_field = grad_out + norm_back(grad_normed, normed, spread)
    return (grad_field, cell_sum(normed_b, grad_pre), cell_sum(normed_b, grad_gate))

def triangle(left_proj, right_proj, outgoing):
    left_wide = left_proj.astype(jnp.float32)
    right_wide = right_proj.astype(jnp.float32)
    if outgoing:
        return jnp.einsum('ikh,jkh->ijh', left_wide, right_wide, precision=lax.Precision.HIGHEST)
    return jnp.einsum('kih,kjh->ijh', left_wide, right_wide, precision=lax.Precision.HIGHEST)

def triangle_back(grad_tri, left_proj, right_proj, outgoing):
    grad_wide = grad_tri.astype(jnp.float32)
    left_wide = left_proj.astype(jnp.float32)
    right_wide = right_proj.astype(jnp.float32)
    if outgoing:
        grad_left = jnp.einsum('ijh,jkh->ikh', grad_wide, right_wide, precision=lax.Precision.HIGHEST)
        grad_right = jnp.einsum('ijh,ikh->jkh', grad_wide, left_wide, precision=lax.Precision.HIGHEST)
    else:
        grad_left = jnp.einsum('ijh,kjh->kih', grad_wide, right_wide, precision=lax.Precision.HIGHEST)
        grad_right = jnp.einsum('ijh,kih->kjh', grad_wide, left_wide, precision=lax.Precision.HIGHEST)
    return (grad_left, grad_right)

def module_pass(pair_field, grad_source, w_proj, w_gate, w_lift, outgoing):
    normed, spread, normed_b, pre_act, left_proj, right_proj, gate_val = project_tile(pair_field, w_proj, w_gate)
    tri_sum = triangle(left_proj, right_proj, outgoing)
    update, unit, unit_spread, unit_b, lifted = finish_tile(tri_sum, gate_val, w_lift)
    saved = (normed, spread, normed_b, pre_act, left_proj, right_proj, gate_val, unit, unit_spread, unit_b, lifted)
    return (pair_field + update, saved)

def module_back(grad_out, saved, w_proj, w_gate, w_lift, outgoing):
    normed, spread, normed_b, pre_act, left_proj, right_proj, gate_val, unit, unit_spread, unit_b, lifted = saved
    grad_tri, grad_gate, dlift = head_back(grad_out, gate_val, lifted, unit, unit_spread, unit_b, w_lift)
    grad_left, grad_right = triangle_back(grad_tri, left_proj, right_proj, outgoing)
    grad_field, dproj, dgate = tail_back(grad_out, grad_gate, grad_left, grad_right, normed, spread, normed_b, pre_act, w_proj, w_gate)
    return (grad_field, dproj, dgate, dlift)

def reference(pair_in, cotangent, outgoing_proj, outgoing_gate, outgoing_lift, incoming_proj, incoming_gate, incoming_lift):
    middle, saved_out = module_pass(pair_in, None, outgoing_proj, outgoing_gate, outgoing_lift, True)
    pair_result, saved_inc = module_pass(middle, None, incoming_proj, incoming_gate, incoming_lift, False)
    grad_middle, dproj_inc, dgate_inc, dlift_inc = module_back(cotangent, saved_inc, incoming_proj, incoming_gate, incoming_lift, False)
    pair_grad, dproj_out, dgate_out, dlift_out = module_back(grad_middle, saved_out, outgoing_proj, outgoing_gate, outgoing_lift, True)
    return (pair_result, pair_grad, dproj_out, dgate_out, dlift_out, dproj_inc, dgate_inc, dlift_inc)
```

```python
import types

import jax
import jax.numpy as jnp
from jax import lax
from jax.experimental import pallas as pl
from jax.experimental.pallas import tpu as pltpu
from jax.sharding import PartitionSpec as P

F32 = jnp.float32
BF16 = jnp.bfloat16
EPSILON = 1e-05
MESH = pl.DeviceIdType.MESH

ROWS, COLS, DEVICES = 16, 8, 128
BI, BK, C = 24, 48, 128
TILES = 12
SLOT = 64
WIDE = COLS * SLOT
CELLS = TILES * 128
DBL, SGL, GRD = 24, 16, 8

MODULE_FIELDS = ("n", "s1", "p2", "s3", "p4", "gate", "u", "lifted")
FLAT_FIELDS = ("nb", "ub", "gl", "gg")


def dot(a, b, ca=1, cb=0):
    return lax.dot_general(a, b, (((ca,), (cb,)), ((), ())), preferred_element_type=F32)


def norm(p):
    d = p - jnp.mean(p, axis=0, keepdims=True)
    r = lax.rsqrt(jnp.mean(d * d, axis=0, keepdims=True) + EPSILON)
    return d * r, r


def norm_back(q, n, r):
    return (q - jnp.mean(q, axis=0, keepdims=True) - n * jnp.mean(q * n, axis=0, keepdims=True)) * r


def lanes(t):
    return pl.ds(pl.multiple_of(t * 128, 128), 128)


def kernel(*refs):
    (pair, cot, wp_o, wg_o, wl_o, wp_i, wg_i, wl_i, res, grad, dpo, dgo, dlo, dpi, dgi, dli) = refs[:16]
    it = iter(refs[16:])

    def module(wp, wg, wl):
        m = types.SimpleNamespace(wp=wp, wg=wg, wl=wl)
        for name in MODULE_FIELDS + FLAT_FIELDS + ("gp", "r", "ur", "wpt", "wgt", "wlt", "ml", "mr", "ws", "wr", "wa"):
            setattr(m, name, next(it))
        return m

    out, inc = module(wp_o, wg_o, wl_o), module(wp_i, wg_i, wl_i)
    xt, ct, mt, gt, stage, gmat, snd_d, rec_d, snd_s, rec_s, ssem, rsem = it

    row, col = lax.axis_index("row"), lax.axis_index("col")
    me = row * COLS + col
    cols = [lax.rem(col + b, COLS) for b in range(COLS)]

    def peers(visit):
        def step(a, carry):
            rr = lax.rem(row + a, ROWS)
            for b in range(COLS):
                if b:
                    visit(rr, cols[b])
                else:
                    @pl.when(a > 0)
                    def _():
                        visit(rr, cols[0])
            return carry

        lax.fori_loop(0, ROWS, step, 0)

    barrier = pltpu.get_barrier_semaphore()
    peers(lambda rr, cc: pl.semaphore_signal(barrier, inc=1, device_id=(rr, cc), device_id_type=MESH))

    def start(src, dst, k, rr, cc):
        pltpu.make_async_remote_copy(
            src, dst, ssem.at[k], rsem.at[k], device_id=(rr, cc), device_id_type=MESH
        ).start()

    def drain(ref, sem, k):
        span = ref.at[pl.ds(0, DEVICES - 1)]
        pltpu.make_async_copy(span, span, sem.at[k]).wait()

    def arrive(ref, k):
        drain(ref, rsem, k)

    def send_staged(snd, dst, k, size):
        def piece(p):
            return stage[pl.ds(pl.multiple_of(p * size, 8), size), :].astype(BF16)

        def visit(rr, cc):
            p = rr * COLS + cc
            snd[p] = piece(p)
            start(snd.at[p], dst.at[me], k, rr, cc)

        peers(visit)
        dst[me] = piece(me)

    def send_ready(snd, dst, k):
        peers(lambda rr, cc: start(snd.at[rr * COLS + cc], dst.at[me], k, rr, cc))
        dst[me] = snd[me]

    def unpack(rec, size):
        def step(a, carry):
            for b in range(COLS):
                p = a * COLS + b
                stage[pl.ds(pl.multiple_of(p * size, 8), size), :] = rec[p].astype(F32)
            return carry

        lax.fori_loop(0, ROWS, step, 0)

    def tiles(body):
        lax.fori_loop(0, TILES, lambda t, carry: (body(t), carry)[1], 0)

    low = lax.broadcasted_iota(jnp.int32, (BI, 128), 1) < SLOT
    top = lax.broadcasted_iota(jnp.int32, (BI, 128), 0) < TILES
    gap8 = jnp.zeros((8, 128), F32)
    gap16 = jnp.zeros((16, 128), F32)

    def swap_lanes(a):
        return pltpu.roll(a, SLOT, 1)

    def swap_rows(a):
        return pltpu.roll(a, TILES, 0)

    def halves(a, b):
        return jnp.where(low, a, swap_lanes(b)), jnp.where(low, swap_lanes(a), b)

    def assemble_double(rec, left, right):
        def step(r2, carry):
            at = pl.ds(pl.multiple_of(r2 * SLOT, SLOT), SLOT)
            for m in range(COLS // 2):
                ls, rs = [], []
                for s in range(2):
                    p = (2 * r2 + s) * COLS + 2 * m
                    o0, o1 = halves(rec[p].astype(F32), rec[p + 1].astype(F32))
                    ls.append(jnp.where(top, o0, swap_rows(o1)))
                    rs.append(jnp.where(top, swap_rows(o0), o1))
                left[at, m * 128 : (m + 1) * 128] = jnp.concatenate(ls + [gap16], axis=0).astype(BF16)
                right[at, m * 128 : (m + 1) * 128] = jnp.concatenate(rs + [gap16], axis=0).astype(BF16)
            return carry

        lax.fori_loop(0, ROWS // 2, step, 0)

    def assemble_single(rec, whole):
        def step(r2, carry):
            at = pl.ds(pl.multiple_of(r2 * SLOT, SLOT), SLOT)
            for m in range(COLS // 2):
                ls = []
                for s in range(2):
                    p = (2 * r2 + s) * COLS + 2 * m
                    a, b = (jnp.concatenate([rec[q].astype(F32), gap8], axis=0) for q in (p, p + 1))
                    o0, o1 = halves(a, b)
                    ls.append(jnp.where(top, o0, swap_rows(o1)))
                whole[at, m * 128 : (m + 1) * 128] = jnp.concatenate(ls + [gap16], axis=0).astype(BF16)
            return carry

        lax.fori_loop(0, ROWS // 2, step, 0)

    def cut(block, upper):
        turned = swap_rows(block)
        first, second = (turned, block) if upper else (block, turned)
        return jnp.where(low, first, swap_lanes(second)), jnp.where(low, swap_lanes(first), second)

    def split_rows(rows_of, snd):
        def step(q, carry):
            blocks = rows_of(pl.ds(pl.multiple_of(q * 128, 128), 128))
            for s4 in range(4):
                lo = SLOT * (s4 // 2) + BI * (s4 % 2)
                for m in range(COLS // 2):
                    p = (4 * q + s4) * COLS + 2 * m
                    ms = [cut(b[lo : lo + BI, m * 128 : (m + 1) * 128], j) for j, b in enumerate(blocks)]
                    if len(ms) == 1:
                        snd[p] = ms[0][0][:SGL].astype(BF16)
                        snd[p + 1] = ms[0][1][:SGL].astype(BF16)
                    else:
                        snd[p] = jnp.where(top, ms[0][0], ms[1][0]).astype(BF16)
                        snd[p + 1] = jnp.where(top, ms[0][1], ms[1][1]).astype(BF16)
            return carry

        lax.fori_loop(0, WIDE // 128, step, 0)

    def into_tiles(src, dst):
        def body(t):
            rows = jnp.concatenate([src[t], gap16, src[TILES + t], gap16], axis=0)
            dst[t] = rows.T

        tiles(body)

    def out_tile(t, value, dst):
        back = value.T
        dst[t] = back[:BK]
        dst[TILES + t] = back[SLOT : SLOT + BK]

    def strided(t, size):
        return stage[pl.ds(t, 128, stride=size), :]

    def project(t, x, m):
        n, r = norm(x)
        nb = n.astype(BF16)
        m.n[t] = n
        m.r[t] = jnp.broadcast_to(r, (8, 128))
        m.nb[:, lanes(t)] = nb
        wpt = m.wpt
        s1 = jax.nn.sigmoid(dot(wpt[0:128], nb))
        p2 = dot(wpt[128:256], nb)
        m.s1[t] = s1
        m.p2[t] = p2
        stage[pl.ds(t, 128, stride=DBL), :] = s1 * p2
        s3 = jax.nn.sigmoid(dot(wpt[256:384], nb))
        p4 = dot(wpt[384:512], nb)
        m.s3[t] = s3
        m.p4[t] = p4
        stage[pl.ds(TILES + t, 128, stride=DBL), :] = s3 * p4
        m.gate[t] = jax.nn.sigmoid(dot(m.wgt[...], nb))

    def finish(t, tri, base, m):
        u, r = norm(tri)
        ub = u.astype(BF16)
        m.u[t] = u
        m.ur[t] = jnp.broadcast_to(r, (8, 128))
        m.ub[:, lanes(t)] = ub
        lifted = dot(m.wlt[...], ub)
        m.lifted[t] = lifted
        return base + m.gate[t] * lifted

    def head_back(t, g, m):
        gate = m.gate[t]
        through = g * gate
        gl = through.astype(BF16)
        m.gl[:, lanes(t)] = gl
        m.gg[:, lanes(t)] = (through * m.lifted[t] * (1.0 - gate)).astype(BF16)
        gunit = dot(m.wl[...], gl)
        stage[pl.ds(t, 128, stride=SGL), :] = norm_back(gunit, m.u[t], m.ur[t][0:1])

    def pre_back(t, m):
        gl, gr = strided(t, DBL), strided(TILES + t, DBL)
        s1, s3 = m.s1[t], m.s3[t]
        a, b = gl * s1, gr * s3
        m.gp[0:128, lanes(t)] = (a * m.p2[t] * (1.0 - s1)).astype(BF16)
        m.gp[128:256, lanes(t)] = a.astype(BF16)
        m.gp[256:384, lanes(t)] = (b * m.p4[t] * (1.0 - s3)).astype(BF16)
        m.gp[384:512, lanes(t)] = b.astype(BF16)

    def tail_back(t, g, m):
        gn = dot(m.wp[...], m.gp[:, lanes(t)]) + dot(m.wg[...], m.gg[:, lanes(t)])
        return g + norm_back(gn, m.n[t], m.r[t][0:1])

    def weight_rows(m, j, value):
        m.ws[pl.ds(j, 128, stride=GRD), :] = value

    def small_grads(m):
        weight_rows(m, 4, dot(m.nb[...], m.gg[...], 1, 1))
        weight_rows(m, 5, dot(m.ub[...], m.gl[...], 1, 1))

    def proj_grads(m):
        for j in range(4):
            weight_rows(m, j, dot(m.nb[...], m.gp[j * 128 : (j + 1) * 128, :], 1, 1))

    def part(ref, p):
        return ref.at[pl.ds(pl.multiple_of(p * GRD, GRD), GRD)]

    def scatter_grads(m, k):
        peers(lambda rr, cc: start(part(m.ws, rr * COLS + cc), m.wr.at[me], k, rr, cc))
        m.wr[me] = m.ws[pl.ds(pl.multiple_of(me * GRD, GRD), GRD), :]

    def gather_grads(m, k):
        arrive(m.wr, k)
        total = lax.fori_loop(
            0, ROWS, lambda a, acc: acc + jnp.sum(m.wr[pl.ds(a * COLS, COLS)], axis=0), jnp.zeros((GRD, 128), F32)
        )
        m.wa[pl.ds(pl.multiple_of(me * GRD, GRD), GRD), :] = total
        peers(lambda rr, cc: start(part(m.wa, me), part(m.wa, me), k + 1, rr, cc))

    def write_grads(m, k, dp, dg, dl):
        span = m.wa.at[pl.ds(0, (DEVICES - 1) * GRD)]
        pltpu.make_async_copy(span, span, rsem.at[k + 1]).wait()
        for j in range(4):
            dp[:, j * 128 : (j + 1) * 128] = m.wa[pl.ds(j, 128, stride=GRD), :]
        dg[...] = m.wa[pl.ds(4, 128, stride=GRD), :]
        dl[...] = m.wa[pl.ds(5, 128, stride=GRD), :]

    for m in (out, inc):
        m.wpt[...] = m.wp[...].T
        m.wgt[...] = m.wg[...].T
        m.wlt[...] = m.wl[...].T
        m.ws[...] = jnp.zeros(m.ws.shape, F32)
    into_tiles(pair, xt)
    tiles(lambda t: project(t, xt[t], out))
    pl.semaphore_wait(barrier, DEVICES - 1)
    send_staged(snd_d.at[0], rec_d.at[0], 0, DBL)
    into_tiles(cot, ct)
    arrive(rec_d.at[0], 0)
    assemble_double(rec_d.at[0], out.ml, out.mr)
    split_rows(lambda at: [dot(out.ml[at, :], out.mr[...], 1, 1)], snd_s.at[0])
    send_ready(snd_s.at[0], rec_s.at[0], 1)
    arrive(rec_s.at[0], 1)
    unpack(rec_s.at[0], SGL)

    def middle_tile(t):
        mid = finish(t, strided(t, SGL), xt[t], out)
        mt[t] = mid

    tiles(middle_tile)
    tiles(lambda t: project(t, mt[t], inc))
    send_staged(snd_d.at[1], rec_d.at[1], 2, DBL)
    arrive(rec_d.at[1], 2)
    assemble_double(rec_d.at[1], inc.ml, inc.mr)
    split_rows(lambda at: [dot(inc.ml[:, at], inc.mr[...], 0, 0)], snd_s.at[1])
    send_ready(snd_s.at[1], rec_s.at[1], 3)
    arrive(rec_s.at[1], 3)
    unpack(rec_s.at[1], SGL)

    def result_tile(t):
        mt[t] = finish(t, strided(t, SGL), mt[t], inc)
        head_back(t, ct[t], inc)

    tiles(result_tile)
    send_staged(snd_s.at[2], rec_s.at[2], 4, SGL)
    tiles(lambda t: out_tile(t, mt[t], res))
    arrive(rec_s.at[2], 4)
    assemble_single(rec_s.at[2], gmat)
    split_rows(
        lambda at: [dot(inc.mr[at, :], gmat[...], 1, 1), dot(inc.ml[at, :], gmat[...], 1, 0)], snd_d.at[2]
    )
    send_ready(snd_d.at[2], rec_d.at[2], 5)
    small_grads(inc)
    arrive(rec_d.at[2], 5)
    unpack(rec_d.at[2], DBL)

    tiles(lambda t: pre_back(t, inc))

    def grad_middle_tile(t):
        g = tail_back(t, ct[t], inc)
        gt[t] = g
        head_back(t, g, out)

    tiles(grad_middle_tile)
    send_staged(snd_s.at[3], rec_s.at[3], 6, SGL)
    proj_grads(inc)
    scatter_grads(inc, 8)
    arrive(rec_s.at[3], 6)
    assemble_single(rec_s.at[3], gmat)
    split_rows(
        lambda at: [dot(gmat[at, :], out.mr[...], 1, 0), dot(gmat[:, at], out.ml[...], 0, 0)], snd_d.at[3]
    )
    send_ready(snd_d.at[3], rec_d.at[3], 7)
    small_grads(out)
    gather_grads(inc, 8)
    arrive(rec_d.at[3], 7)
    unpack(rec_d.at[3], DBL)
    tiles(lambda t: pre_back(t, out))
    proj_grads(out)
    scatter_grads(out, 10)
    tiles(lambda t: out_tile(t, tail_back(t, gt[t], out), grad))
    write_grads(inc, 8, dpi, dgi, dli)
    gather_grads(out, 10)
    write_grads(out, 10, dpo, dgo, dlo)

    for j, k in enumerate((0, 2, 5, 7)):
        drain(snd_d.at[j], ssem, k)
    for j, k in enumerate((1, 3, 4, 6)):
        drain(snd_s.at[j], ssem, k)
    for m, k in ((inc, 8), (out, 10)):
        drain(m.wr, ssem, k)
        drain(m.wr, ssem, k + 1)


def scratch():
    shapes = []
    for _ in range(2):
        shapes += [pltpu.VMEM((TILES, 128, 128), F32)] * len(MODULE_FIELDS)
        shapes += [pltpu.VMEM((128, CELLS), BF16)] * len(FLAT_FIELDS)
        shapes += [
            pltpu.VMEM((512, CELLS), BF16),
            pltpu.VMEM((TILES, 8, 128), F32),
            pltpu.VMEM((TILES, 8, 128), F32),
            pltpu.VMEM((512, 128), BF16),
            pltpu.VMEM((128, 128), BF16),
            pltpu.VMEM((128, 128), BF16),
            pltpu.VMEM((WIDE, WIDE), BF16),
            pltpu.VMEM((WIDE, WIDE), BF16),
            pltpu.VMEM((DEVICES * GRD, 128), F32),
            pltpu.VMEM((DEVICES, GRD, 128), F32),
            pltpu.VMEM((DEVICES * GRD, 128), F32),
        ]
    shapes += [pltpu.VMEM((TILES, 128, 128), F32)] * 4
    shapes += [
        pltpu.VMEM((DEVICES * DBL, 128), F32),
        pltpu.VMEM((WIDE, WIDE), BF16),
        pltpu.VMEM((4, DEVICES, DBL, 128), BF16),
        pltpu.VMEM((4, DEVICES, DBL, 128), BF16),
        pltpu.VMEM((4, DEVICES, SGL, 128), BF16),
        pltpu.VMEM((4, DEVICES, SGL, 128), BF16),
        pltpu.SemaphoreType.DMA((12,)),
        pltpu.SemaphoreType.DMA((12,)),
    ]
    return shapes


def local(*args):
    vmem = pl.BlockSpec(memory_space=pltpu.VMEM)
    pair = jax.ShapeDtypeStruct((BI, BK, C), F32)
    square = jax.ShapeDtypeStruct((C, C), F32)
    proj = jax.ShapeDtypeStruct((C, 4 * C), F32)
    return pl.pallas_call(
        kernel,
        out_shape=(pair, pair, proj, square, square, proj, square, square),
        in_specs=[vmem] * 8,
        out_specs=(vmem,) * 8,
        scratch_shapes=scratch(),
        compiler_params=pltpu.CompilerParams(
            has_side_effects=True, collective_id=0, vmem_limit_bytes=58 * 2**20
        ),
        name="triangles",
    )(*args)


def solution(mesh):
    specs = (P("row", "col", None), P("row", "col", None), P(), P(), P(), P(), P(), P())
    return jax.shard_map(local, mesh=mesh, in_specs=specs, out_specs=specs, check_vma=False)
```

```python
import types

import jax
import jax.numpy as jnp
from jax import lax
from jax.experimental import pallas as pl
from jax.experimental.pallas import tpu as pltpu
from jax.sharding import PartitionSpec as P

F32 = jnp.float32
BF16 = jnp.bfloat16
EPSILON = 1e-05
MESH = pl.DeviceIdType.MESH

ROWS, COLS, DEVICES = 16, 8, 128
BI, BK, C = 24, 48, 128
TILES = 12
SLOT = 64
WIDE = COLS * SLOT
CELLS = TILES * 128
DBL, SGL = 24, 16
GRD, TAIL = 8, 4
OFFSETS = sorted(
    ((dx, dy, dz, dc) for dx in range(4) for dy in range(4) for dz in range(4) for dc in range(2)),
    key=lambda o: -sum(min(v, 4 - v) for v in o[:3]),
)
OFFSETS.remove((0, 0, 0, 0))

MODULE_FIELDS = ("n", "s1", "p2", "s3", "p4", "gate", "u", "lifted")
FLAT_FIELDS = ("nb", "ub", "gl", "gg")


def dot(a, b, ca=1, cb=0):
    return lax.dot_general(a, b, (((ca,), (cb,)), ((), ())), preferred_element_type=F32)


def norm(p):
    d = p - jnp.mean(p, axis=0, keepdims=True)
    r = lax.rsqrt(jnp.mean(d * d, axis=0, keepdims=True) + EPSILON)
    return d * r, r


def norm_back(q, n, r):
    return (q - jnp.mean(q, axis=0, keepdims=True) - n * jnp.mean(q * n, axis=0, keepdims=True)) * r


def lanes(t):
    return pl.ds(pl.multiple_of(t * 128, 128), 128)


def kernel(*refs):
    (pair, cot, wp_o, wg_o, wl_o, wp_i, wg_i, wl_i, res, grad, dpo, dgo, dlo, dpi, dgi, dli) = refs[:16]
    it = iter(refs[16:])

    def module(wp, wg, wl):
        m = types.SimpleNamespace(wp=wp, wg=wg, wl=wl)
        for name in MODULE_FIELDS + FLAT_FIELDS + ("gp", "r", "ur", "wpt", "wgt", "wlt", "ml", "mr"):
            setattr(m, name, next(it))
        return m

    out, inc = module(wp_o, wg_o, wl_o), module(wp_i, wg_i, wl_i)
    xt, ct, mt, gt, stage, gmat, snd_d, rec_d, snd_s, rec_s = (next(it) for _ in range(10))
    ws, ga, gb, ssem, rsem = next(it), (next(it), next(it), next(it)), (next(it), next(it), next(it)), next(it), next(it)

    row, col = lax.axis_index("row"), lax.axis_index("col")
    me = row * COLS + col
    x = row // 8 * 2 + lax.rem(col, 2)
    xs = [lax.rem(x + d, 4) for d in range(4)]
    row_x = [v // 2 * 8 for v in xs]
    col_x = [lax.rem(v, 2) for v in xs]
    row_z = [lax.rem(lax.rem(row, 8) // 2 + d, 4) * 2 for d in range(4)]
    col_y = [lax.rem(col // 2 + d, 4) * 2 for d in range(4)]
    row_c = [lax.rem(row + d, 2) for d in range(2)]

    def peers(visit):
        for dx, dy, dz, dc in OFFSETS:
            visit(row_x[dx] + row_z[dz] + row_c[dc], col_y[dy] + col_x[dx])

    barrier = pltpu.get_barrier_semaphore()
    peers(lambda rr, cc: pl.semaphore_signal(barrier, inc=1, device_id=(rr, cc), device_id_type=MESH))

    def start(src, dst, k, rr, cc):
        pltpu.make_async_remote_copy(
            src, dst, ssem.at[k], rsem.at[k], device_id=(rr, cc), device_id_type=MESH
        ).start()

    def drain(ref, sem, k):
        span = ref.at[pl.ds(0, DEVICES - 1)]
        pltpu.make_async_copy(span, span, sem.at[k]).wait()

    def arrive(ref, k):
        drain(ref, rsem, k)

    def piece(p, size):
        return stage[pl.ds(pl.multiple_of(p * size, 8), size), :]

    def put(ref, p, value):
        if ref.shape[1:] == (3, 4, 128):
            for j in range(3):
                ref[p, j] = value[4 * j : 4 * j + 4].astype(BF16)
        else:
            ref[p] = value.astype(BF16)

    def send_staged(snd, dst, k, size):
        def visit(rr, cc):
            p = rr * COLS + cc
            put(snd, p, piece(p, size))
            start(snd.at[p], dst.at[me], k, rr, cc)

        peers(visit)
        put(dst, me, piece(me, size))

    def send_ready(snd, dst, k):
        peers(lambda rr, cc: start(snd.at[rr * COLS + cc], dst.at[me], k, rr, cc))
        dst[me] = snd[me]

    def unpack(rec, size):
        def step(a, carry):
            for b in range(COLS):
                p = a * COLS + b
                at = pl.multiple_of(p * size, 8)
                if rec.shape[1:] == (3, 4, 128):
                    for j in range(3):
                        stage[pl.ds(at + 4 * j, 4), :] = rec[p, j].astype(F32)
                else:
                    stage[pl.ds(at, size), :] = rec[p].astype(F32)
            return carry

        lax.fori_loop(0, ROWS, step, 0)

    def tiles(body):
        lax.fori_loop(0, TILES, lambda t, carry: (body(t), carry)[1], 0, unroll=4)

    low = lax.broadcasted_iota(jnp.int32, (BI, 128), 1) < SLOT
    top = lax.broadcasted_iota(jnp.int32, (BI, 128), 0) < TILES
    gap8 = jnp.zeros((8, 128), F32)
    gap16 = jnp.zeros((16, 128), F32)

    def swap_lanes(a):
        return pltpu.roll(a, SLOT, 1)

    def swap_rows(a):
        return pltpu.roll(a, TILES, 0)

    def halves(a, b):
        return jnp.where(low, a, swap_lanes(b)), jnp.where(low, swap_lanes(a), b)

    def assemble_double(rec, left, right):
        def step(r2, carry):
            at = pl.ds(pl.multiple_of(r2 * SLOT, SLOT), SLOT)
            for m in range(COLS // 2):
                ls, rs = [], []
                for s in range(2):
                    p = (2 * r2 + s) * COLS + 2 * m
                    o0, o1 = halves(rec[p].astype(F32), rec[p + 1].astype(F32))
                    ls.append(jnp.where(top, o0, swap_rows(o1)))
                    rs.append(jnp.where(top, swap_rows(o0), o1))
                left[at, m * 128 : (m + 1) * 128] = jnp.concatenate(ls + [gap16], axis=0).astype(BF16)
                right[at, m * 128 : (m + 1) * 128] = jnp.concatenate(rs + [gap16], axis=0).astype(BF16)
            return carry

        lax.fori_loop(0, ROWS // 2, step, 0)

    def assemble_single(rec, whole):
        unpack(rec, SGL)

        def step(r2, carry):
            at = pl.ds(pl.multiple_of(r2 * SLOT, SLOT), SLOT)
            for m in range(COLS // 2):
                ls = []
                for s in range(2):
                    p = (2 * r2 + s) * COLS + 2 * m
                    a, b = (jnp.concatenate([piece(q, SGL), gap8], axis=0) for q in (p, p + 1))
                    o0, o1 = halves(a, b)
                    ls.append(jnp.where(top, o0, swap_rows(o1)))
                whole[at, m * 128 : (m + 1) * 128] = jnp.concatenate(ls + [gap16], axis=0).astype(BF16)
            return carry

        lax.fori_loop(0, ROWS // 2, step, 0)

    def cut(block, upper):
        turned = swap_rows(block)
        first, second = (turned, block) if upper else (block, turned)
        return jnp.where(low, first, swap_lanes(second)), jnp.where(low, swap_lanes(first), second)

    def split_rows(rows_of, snd):
        def step(q, carry):
            blocks = rows_of(pl.ds(pl.multiple_of(q * 128, 128), 128))
            for s4 in range(4):
                lo = SLOT * (s4 // 2) + BI * (s4 % 2)
                for m in range(COLS // 2):
                    p = (4 * q + s4) * COLS + 2 * m
                    ms = [cut(b[lo : lo + BI, m * 128 : (m + 1) * 128], j) for j, b in enumerate(blocks)]
                    if len(ms) == 1:
                        put(snd, p, ms[0][0])
                        put(snd, p + 1, ms[0][1])
                    else:
                        snd[p] = jnp.where(top, ms[0][0], ms[1][0]).astype(BF16)
                        snd[p + 1] = jnp.where(top, ms[0][1], ms[1][1]).astype(BF16)
            return carry

        lax.fori_loop(0, WIDE // 128, step, 0)

    def into_tiles(src, dst):
        def body(t):
            rows = jnp.concatenate([src[t], gap16, src[TILES + t], gap16], axis=0)
            dst[t] = rows.T

        tiles(body)

    def out_tile(t, value, dst):
        back = value.T
        dst[t] = back[:BK]
        dst[TILES + t] = back[SLOT : SLOT + BK]

    def strided(t, size):
        return stage[pl.ds(t, 128, stride=size), :]

    def project(t, x, m):
        n, r = norm(x)
        nb = n.astype(BF16)
        m.n[t] = n
        m.r[t] = jnp.broadcast_to(r, (8, 128))
        m.nb[:, lanes(t)] = nb
        wpt = m.wpt
        s1 = jax.nn.sigmoid(dot(wpt[0:128], nb))
        p2 = dot(wpt[128:256], nb)
        m.s1[t] = s1
        m.p2[t] = p2
        stage[pl.ds(t, 128, stride=DBL), :] = s1 * p2
        s3 = jax.nn.sigmoid(dot(wpt[256:384], nb))
        p4 = dot(wpt[384:512], nb)
        m.s3[t] = s3
        m.p4[t] = p4
        stage[pl.ds(TILES + t, 128, stride=DBL), :] = s3 * p4
        m.gate[t] = jax.nn.sigmoid(dot(m.wgt[...], nb))

    def finish(t, tri, base, m):
        u, r = norm(tri)
        ub = u.astype(BF16)
        m.u[t] = u
        m.ur[t] = jnp.broadcast_to(r, (8, 128))
        m.ub[:, lanes(t)] = ub
        lifted = dot(m.wlt[...], ub)
        m.lifted[t] = lifted
        return base + m.gate[t] * lifted

    def head_back(t, g, m):
        gate = m.gate[t]
        through = g * gate
        gl = through.astype(BF16)
        m.gl[:, lanes(t)] = gl
        m.gg[:, lanes(t)] = (through * m.lifted[t] * (1.0 - gate)).astype(BF16)
        gunit = dot(m.wl[...], gl)
        stage[pl.ds(t, 128, stride=SGL), :] = norm_back(gunit, m.u[t], m.ur[t][0:1])

    def pre_back(t, m):
        gl, gr = strided(t, DBL), strided(TILES + t, DBL)
        s1, s3 = m.s1[t], m.s3[t]
        a, b = gl * s1, gr * s3
        m.gp[0:128, lanes(t)] = (a * m.p2[t] * (1.0 - s1)).astype(BF16)
        m.gp[128:256, lanes(t)] = a.astype(BF16)
        m.gp[256:384, lanes(t)] = (b * m.p4[t] * (1.0 - s3)).astype(BF16)
        m.gp[384:512, lanes(t)] = b.astype(BF16)

    def tail_back(t, g, m):
        gn = dot(m.wp[...], m.gp[:, lanes(t)]) + dot(m.wg[...], m.gg[:, lanes(t)])
        return g + norm_back(gn, m.n[t], m.r[t][0:1])

    def rows_of_grads(j, size, value):
        ws[pl.ds(j, 128, stride=size), :] = value

    def proj_grads(m, size):
        for j in range(4):
            rows_of_grads(j, size, dot(m.nb[...], m.gp[j * 128 : (j + 1) * 128, :], 1, 1))

    def pack_grads(snd, size):
        def step(a, carry):
            for b in range(COLS):
                at = pl.multiple_of(a * (COLS * size), 8) + b * size
                snd[a * COLS + b] = ws[pl.ds(at, size), :].astype(BF16)
            return carry

        lax.fori_loop(0, ROWS, step, 0)

    def sum_grads(rec, whole, size):
        whole[me] = lax.fori_loop(
            0,
            ROWS,
            lambda a, acc: acc + jnp.sum(rec[pl.ds(a * COLS, COLS)].astype(F32), axis=0),
            jnp.zeros((size, 128), F32),
        ).astype(BF16)

    def spread_grads(whole, k):
        peers(lambda rr, cc: start(whole.at[me], whole.at[me], k, rr, cc))

    def unpack_grads(whole, size):
        def step(a, carry):
            for b in range(COLS):
                at = pl.multiple_of(a * (COLS * size), 8) + b * size
                ws[pl.ds(at, size), :] = whole[a * COLS + b].astype(F32)
            return carry

        lax.fori_loop(0, ROWS, step, 0)

    def write_rows(j, size, dst):
        dst[...] = ws[pl.ds(j, 128, stride=size), :]

    for m in (out, inc):
        m.wpt[...] = m.wp[...].T
        m.wgt[...] = m.wg[...].T
        m.wlt[...] = m.wl[...].T
    into_tiles(pair, xt)
    tiles(lambda t: project(t, xt[t], out))
    pl.semaphore_wait(barrier, DEVICES - 1)
    send_staged(snd_d.at[0], rec_d.at[0], 0, DBL)
    into_tiles(cot, ct)
    arrive(rec_d.at[0], 0)
    assemble_double(rec_d.at[0], out.ml, out.mr)
    split_rows(lambda at: [dot(out.ml[at, :], out.mr[...], 1, 1)], snd_s.at[0])
    send_ready(snd_s.at[0], rec_s.at[0], 1)
    arrive(rec_s.at[0], 1)
    unpack(rec_s.at[0], SGL)

    def middle_tile(t):
        mid = finish(t, strided(t, SGL), xt[t], out)
        mt[t] = mid

    tiles(middle_tile)
    tiles(lambda t: project(t, mt[t], inc))
    send_staged(snd_d.at[1], rec_d.at[1], 2, DBL)
    arrive(rec_d.at[1], 2)
    assemble_double(rec_d.at[1], inc.ml, inc.mr)
    split_rows(lambda at: [dot(inc.ml[:, at], inc.mr[...], 0, 0)], snd_s.at[1])
    send_ready(snd_s.at[1], rec_s.at[1], 3)
    arrive(rec_s.at[1], 3)
    unpack(rec_s.at[1], SGL)

    def result_tile(t):
        mt[t] = finish(t, strided(t, SGL), mt[t], inc)
        head_back(t, ct[t], inc)

    tiles(result_tile)
    send_staged(snd_s.at[2], rec_s.at[2], 4, SGL)
    tiles(lambda t: out_tile(t, mt[t], res))
    arrive(rec_s.at[2], 4)
    assemble_single(rec_s.at[2], gmat)
    split_rows(
        lambda at: [dot(inc.mr[at, :], gmat[...], 1, 1), dot(inc.ml[at, :], gmat[...], 1, 0)], snd_d.at[2]
    )
    send_ready(snd_d.at[2], rec_d.at[2], 5)
    arrive(rec_d.at[2], 5)
    unpack(rec_d.at[2], DBL)

    tiles(lambda t: pre_back(t, inc))

    def grad_middle_tile(t):
        g = tail_back(t, ct[t], inc)
        gt[t] = g
        head_back(t, g, out)

    tiles(grad_middle_tile)
    send_staged(snd_s.at[3], rec_s.at[3], 6, SGL)
    proj_grads(inc, GRD)
    rows_of_grads(4, GRD, dot(inc.nb[...], inc.gg[...], 1, 1))
    rows_of_grads(5, GRD, dot(inc.ub[...], inc.gl[...], 1, 1))
    rows_of_grads(6, GRD, dot(out.nb[...], out.gg[...], 1, 1))
    rows_of_grads(7, GRD, dot(out.ub[...], out.gl[...], 1, 1))
    pack_grads(ga[0], GRD)
    arrive(rec_s.at[3], 6)
    send_ready(ga[0], ga[1], 8)
    assemble_single(rec_s.at[3], gmat)
    split_rows(
        lambda at: [dot(gmat[at, :], out.mr[...], 1, 0), dot(gmat[:, at], out.ml[...], 0, 0)], snd_d.at[3]
    )
    send_ready(snd_d.at[3], rec_d.at[3], 7)
    arrive(ga[1], 8)
    sum_grads(ga[1], ga[2], GRD)
    arrive(rec_d.at[3], 7)
    spread_grads(ga[2], 9)
    unpack(rec_d.at[3], DBL)
    tiles(lambda t: pre_back(t, out))
    proj_grads(out, TAIL)
    pack_grads(gb[0], TAIL)
    send_ready(gb[0], gb[1], 10)
    tiles(lambda t: out_tile(t, tail_back(t, gt[t], out), grad))
    arrive(gb[1], 10)
    sum_grads(gb[1], gb[2], TAIL)
    spread_grads(gb[2], 11)
    arrive(ga[2], 9)
    unpack_grads(ga[2], GRD)
    for j in range(4):
        write_rows(j, GRD, dpi.at[:, j * 128 : (j + 1) * 128])
    for j, dst in ((4, dgi), (5, dli), (6, dgo), (7, dlo)):
        write_rows(j, GRD, dst)
    arrive(gb[2], 11)
    unpack_grads(gb[2], TAIL)
    for j in range(4):
        write_rows(j, TAIL, dpo.at[:, j * 128 : (j + 1) * 128])

    for j, k in enumerate((0, 2, 5, 7)):
        drain(snd_d.at[j], ssem, k)
    for j, k in enumerate((1, 3, 4, 6)):
        drain(snd_s.at[j], ssem, k)
    for g, k in ((ga, 8), (gb, 10)):
        drain(g[0], ssem, k)
        drain(g[2], ssem, k + 1)


def scratch():
    shapes = []
    for _ in range(2):
        shapes += [pltpu.VMEM((TILES, 128, 128), F32)] * len(MODULE_FIELDS)
        shapes += [pltpu.VMEM((128, CELLS), BF16)] * len(FLAT_FIELDS)
        shapes += [
            pltpu.VMEM((512, CELLS), BF16),
            pltpu.VMEM((TILES, 8, 128), F32),
            pltpu.VMEM((TILES, 8, 128), F32),
            pltpu.VMEM((512, 128), BF16),
            pltpu.VMEM((128, 128), BF16),
            pltpu.VMEM((128, 128), BF16),
            pltpu.VMEM((WIDE, WIDE), BF16),
            pltpu.VMEM((WIDE, WIDE), BF16),
        ]
    shapes += [pltpu.VMEM((TILES, 128, 128), F32)] * 4
    shapes += [
        pltpu.VMEM((DEVICES * DBL, 128), F32),
        pltpu.VMEM((WIDE, WIDE), BF16),
        pltpu.VMEM((4, DEVICES, DBL, 128), BF16),
        pltpu.VMEM((4, DEVICES, DBL, 128), BF16),
        pltpu.VMEM((4, DEVICES, 3, 4, 128), BF16),
        pltpu.VMEM((4, DEVICES, 3, 4, 128), BF16),
        pltpu.VMEM((DEVICES * GRD, 128), F32),
    ]
    shapes += [pltpu.VMEM((DEVICES, GRD, 128), BF16)] * 3
    shapes += [pltpu.VMEM((DEVICES, TAIL, 128), BF16)] * 3
    shapes += [
        pltpu.SemaphoreType.DMA((12,)),
        pltpu.SemaphoreType.DMA((12,)),
    ]
    return shapes


def local(*args):
    vmem = pl.BlockSpec(memory_space=pltpu.VMEM)
    pair = jax.ShapeDtypeStruct((BI, BK, C), F32)
    square = jax.ShapeDtypeStruct((C, C), F32)
    proj = jax.ShapeDtypeStruct((C, 4 * C), F32)
    return pl.pallas_call(
        kernel,
        out_shape=(pair, pair, proj, square, square, proj, square, square),
        in_specs=[vmem] * 8,
        out_specs=(vmem,) * 8,
        scratch_shapes=scratch(),
        compiler_params=pltpu.CompilerParams(
            has_side_effects=True, collective_id=0, vmem_limit_bytes=58 * 2**20
        ),
        name="triangles",
    )(*args)


def solution(mesh):
    specs = (P("row", "col", None), P("row", "col", None), P(), P(), P(), P(), P(), P())
    return jax.shard_map(local, mesh=mesh, in_specs=specs, out_specs=specs, check_vma=False)
```

```python
import types

import jax
import jax.numpy as jnp
from jax import lax
from jax.experimental import pallas as pl
from jax.experimental.pallas import tpu as pltpu
from jax.sharding import PartitionSpec as P

F32 = jnp.float32
BF16 = jnp.bfloat16
EPSILON = 1e-05
MESH = pl.DeviceIdType.MESH

ROWS, COLS, DEVICES = 16, 8, 128
BI, BK, C = 24, 48, 128
TILES = 12
SLOT = 64
WIDE = COLS * SLOT
CELLS = TILES * 128
SGL = 16
GRD, TAIL = 8, 4
OFFSETS = sorted(
    ((dx, dy, dz, dc) for dx in range(4) for dy in range(4) for dz in range(4) for dc in range(2)),
    key=lambda o: -sum(min(v, 4 - v) for v in o[:3]),
)
OFFSETS.remove((0, 0, 0, 0))

MODULE_FIELDS = ("n", "s1", "p2", "s3", "p4", "gate", "u", "lifted")
FLAT_FIELDS = ("nb", "ub", "gl", "gg")


def dot(a, b, ca=1, cb=0):
    return lax.dot_general(a, b, (((ca,), (cb,)), ((), ())), preferred_element_type=F32)


def norm(p):
    d = p - jnp.mean(p, axis=0, keepdims=True)
    r = lax.rsqrt(jnp.mean(d * d, axis=0, keepdims=True) + EPSILON)
    return d * r, r


def norm_back(q, n, r):
    return (q - jnp.mean(q, axis=0, keepdims=True) - n * jnp.mean(q * n, axis=0, keepdims=True)) * r


def lanes(t):
    return pl.ds(pl.multiple_of(t * 128, 128), 128)


def kernel(*refs):
    (pair, cot, wp_o, wg_o, wl_o, wp_i, wg_i, wl_i, res, grad, dpo, dgo, dlo, dpi, dgi, dli) = refs[:16]
    it = iter(refs[16:])

    def module(wp, wg, wl):
        m = types.SimpleNamespace(wp=wp, wg=wg, wl=wl)
        for name in MODULE_FIELDS + FLAT_FIELDS + ("gp", "r", "ur", "wpt", "wgt", "wlt", "ml", "mr"):
            setattr(m, name, next(it))
        return m

    out, inc = module(wp_o, wg_o, wl_o), module(wp_i, wg_i, wl_i)
    xt, ct, mt, gt, stage, gmat, snd, rec, res_v, grad_v = (next(it) for _ in range(10))
    ws, ga, gb, ssem, rsem = next(it), (next(it), next(it), next(it)), (next(it), next(it), next(it)), next(it), next(it)
    osem = next(it)

    row, col = lax.axis_index("row"), lax.axis_index("col")
    me = row * COLS + col
    x = row // 8 * 2 + lax.rem(col, 2)
    xs = [lax.rem(x + d, 4) for d in range(4)]
    row_x = [v // 2 * 8 for v in xs]
    col_x = [lax.rem(v, 2) for v in xs]
    row_z = [lax.rem(lax.rem(row, 8) // 2 + d, 4) * 2 for d in range(4)]
    col_y = [lax.rem(col // 2 + d, 4) * 2 for d in range(4)]
    row_c = [lax.rem(row + d, 2) for d in range(2)]

    def peers(visit):
        for dx, dy, dz, dc in OFFSETS:
            visit(row_x[dx] + row_z[dz] + row_c[dc], col_y[dy] + col_x[dx])

    barrier = pltpu.get_barrier_semaphore()
    peers(lambda rr, cc: pl.semaphore_signal(barrier, inc=1, device_id=(rr, cc), device_id_type=MESH))

    def start(src, dst, k, rr, cc):
        pltpu.make_async_remote_copy(
            src, dst, ssem.at[k], rsem.at[k], device_id=(rr, cc), device_id_type=MESH
        ).start()

    def drain(ref, sem, k):
        span = ref.at[pl.ds(0, DEVICES - 1)]
        pltpu.make_async_copy(span, span, sem.at[k]).wait()

    def arrive(ref, k):
        drain(ref, rsem, k)

    def piece(p):
        return stage[pl.ds(pl.multiple_of(p * SGL, SGL), SGL), :]

    def put(ref, p, value):
        for j in range(3):
            ref[p, j] = value[4 * j : 4 * j + 4].astype(BF16)

    def send_staged(k):
        def visit(rr, cc):
            p = rr * COLS + cc
            put(snd.at[k], p, piece(p))
            start(snd.at[k, p], rec.at[k, me], k, rr, cc)

        peers(visit)
        put(rec.at[k], me, piece(me))

    def send_ready(src, dst, k):
        peers(lambda rr, cc: start(src.at[rr * COLS + cc], dst.at[me], k, rr, cc))
        dst[me] = src[me]

    def unpack(k):
        def step(a, carry):
            for b in range(COLS):
                p = a * COLS + b
                for j in range(3):
                    stage[pl.ds(pl.multiple_of(p * SGL, SGL) + 4 * j, 4), :] = rec[k, p, j].astype(F32)
            return carry

        lax.fori_loop(0, ROWS, step, 0)

    def tiles(body):
        lax.fori_loop(0, TILES, lambda t, carry: (body(t), carry)[1], 0, unroll=4)

    low = lax.broadcasted_iota(jnp.int32, (BI, 128), 1) < SLOT
    top = lax.broadcasted_iota(jnp.int32, (BI, 128), 0) < TILES
    gap8 = jnp.zeros((8, 128), F32)
    gap16 = jnp.zeros((16, 128), F32)

    def swap_lanes(a):
        return pltpu.roll(a, SLOT, 1)

    def swap_rows(a):
        return pltpu.roll(a, TILES, 0)

    def halves(a, b):
        return jnp.where(low, a, swap_lanes(b)), jnp.where(low, swap_lanes(a), b)

    def assemble(k, whole):
        unpack(k)

        def step(r2, carry):
            at = pl.ds(pl.multiple_of(r2 * SLOT, SLOT), SLOT)
            for m in range(COLS // 2):
                ls = []
                for s in range(2):
                    p = (2 * r2 + s) * COLS + 2 * m
                    a, b = (jnp.concatenate([piece(q), gap8], axis=0) for q in (p, p + 1))
                    o0, o1 = halves(a, b)
                    ls.append(jnp.where(top, o0, swap_rows(o1)))
                whole[at, m * 128 : (m + 1) * 128] = jnp.concatenate(ls + [gap16], axis=0).astype(BF16)
            return carry

        lax.fori_loop(0, ROWS // 2, step, 0)

    half = row // 4

    def send_rows(rows_of, k):
        def step(i, carry):
            q = lax.rem(half // 2 + 1 + i // 2, 2) * 2 + lax.rem(half + 1 + i, 2)
            block = rows_of(pl.ds(pl.multiple_of(q * 128, 128), 128))
            for s4 in range(4):
                lo = SLOT * (s4 // 2) + BI * (s4 % 2)
                for m in range(COLS // 2):
                    p = (4 * q + s4) * COLS + 2 * m
                    first = block[lo : lo + BI, m * 128 : (m + 1) * 128]
                    a, b = halves(first, swap_rows(first))
                    put(snd.at[k], p, a)
                    put(snd.at[k], p + 1, b)
            for d in (2, 1, 3, 0):
                for s4 in range(4):
                    for x_lo in range(2):
                        rr, cc = 4 * q + s4, col_y[d] + x_lo
                        p = rr * COLS + cc
                        if d:
                            start(snd.at[k, p], rec.at[k, me], k, rr, cc)
                        else:
                            @pl.when(p != me)
                            def _():
                                start(snd.at[k, p], rec.at[k, me], k, rr, cc)
            return carry

        lax.fori_loop(0, WIDE // 128, step, 0)
        rec[k, me] = snd[k, me]

    def into_tiles(src, dst):
        def body(t):
            rows = jnp.concatenate([src[t], gap16, src[TILES + t], gap16], axis=0)
            dst[t] = rows.T

        tiles(body)

    def out_tile(t, value, dst):
        back = value.T
        dst[t] = back[:BK]
        dst[TILES + t] = back[SLOT : SLOT + BK]

    def strided(t):
        return stage[pl.ds(t, 128, stride=SGL), :]

    def put_strided(t, value):
        stage[pl.ds(t, 128, stride=SGL), :] = value

    def project_left(t, x, m):
        n, r = norm(x)
        nb = n.astype(BF16)
        m.n[t] = n
        m.r[t] = jnp.broadcast_to(r, (8, 128))
        m.nb[:, lanes(t)] = nb
        s1 = jax.nn.sigmoid(dot(m.wpt[0:128], nb))
        p2 = dot(m.wpt[128:256], nb)
        m.s1[t] = s1
        m.p2[t] = p2
        put_strided(t, s1 * p2)

    def project_right(t, m):
        nb = m.nb[:, lanes(t)]
        s3 = jax.nn.sigmoid(dot(m.wpt[256:384], nb))
        p4 = dot(m.wpt[384:512], nb)
        m.s3[t] = s3
        m.p4[t] = p4
        put_strided(t, s3 * p4)

    def project_gate(t, m):
        m.gate[t] = jax.nn.sigmoid(dot(m.wgt[...], m.nb[:, lanes(t)]))

    def finish(t, tri, base, m):
        u, r = norm(tri)
        ub = u.astype(BF16)
        m.u[t] = u
        m.ur[t] = jnp.broadcast_to(r, (8, 128))
        m.ub[:, lanes(t)] = ub
        lifted = dot(m.wlt[...], ub)
        m.lifted[t] = lifted
        return base + m.gate[t] * lifted

    def head_back(t, g, m):
        gate = m.gate[t]
        through = g * gate
        gl = through.astype(BF16)
        m.gl[:, lanes(t)] = gl
        m.gg[:, lanes(t)] = (through * m.lifted[t] * (1.0 - gate)).astype(BF16)
        gunit = dot(m.wl[...], gl)
        put_strided(t, norm_back(gunit, m.u[t], m.ur[t][0:1]))

    def pre_back_left(t, m):
        s1 = m.s1[t]
        a = strided(t) * s1
        m.gp[0:128, lanes(t)] = (a * m.p2[t] * (1.0 - s1)).astype(BF16)
        m.gp[128:256, lanes(t)] = a.astype(BF16)

    def pre_back_right(t, m):
        s3 = m.s3[t]
        b = strided(t) * s3
        m.gp[256:384, lanes(t)] = (b * m.p4[t] * (1.0 - s3)).astype(BF16)
        m.gp[384:512, lanes(t)] = b.astype(BF16)

    def tail_back(t, g, m):
        gn = dot(m.wp[...], m.gp[:, lanes(t)]) + dot(m.wg[...], m.gg[:, lanes(t)])
        return g + norm_back(gn, m.n[t], m.r[t][0:1])

    def rows_of_grads(j, size, value):
        ws[pl.ds(j, 128, stride=size), :] = value

    def proj_grads(m, size):
        for j in range(4):
            rows_of_grads(j, size, dot(m.nb[...], m.gp[j * 128 : (j + 1) * 128, :], 1, 1))

    def pack_grads(snd, size):
        def step(a, carry):
            for b in range(COLS):
                at = pl.multiple_of(a * (COLS * size), 8) + b * size
                snd[a * COLS + b] = ws[pl.ds(at, size), :].astype(BF16)
            return carry

        lax.fori_loop(0, ROWS, step, 0)

    def sum_grads(rec, whole, size):
        whole[me] = lax.fori_loop(
            0,
            ROWS,
            lambda a, acc: acc + jnp.sum(rec[pl.ds(a * COLS, COLS)].astype(F32), axis=0),
            jnp.zeros((size, 128), F32),
        ).astype(BF16)

    def spread_grads(whole, k):
        peers(lambda rr, cc: start(whole.at[me], whole.at[me], k, rr, cc))

    def unpack_grads(whole, size):
        def step(a, carry):
            for b in range(COLS):
                at = pl.multiple_of(a * (COLS * size), 8) + b * size
                ws[pl.ds(at, size), :] = whole[a * COLS + b].astype(F32)
            return carry

        lax.fori_loop(0, ROWS, step, 0)

    def write_rows(j, size, dst):
        dst[...] = ws[pl.ds(j, 128, stride=size), :]

    for m in (out, inc):
        m.wpt[...] = m.wp[...].T
        m.wgt[...] = m.wg[...].T
        m.wlt[...] = m.wl[...].T
    into_tiles(pair, xt)
    tiles(lambda t: project_left(t, xt[t], out))
    pl.semaphore_wait(barrier, DEVICES - 1)
    send_staged(0)
    tiles(lambda t: project_right(t, out))
    send_staged(1)
    tiles(lambda t: project_gate(t, out))
    into_tiles(cot, ct)
    arrive(rec.at[0], 0)
    assemble(0, out.ml)
    arrive(rec.at[1], 1)
    assemble(1, out.mr)
    send_rows(lambda at: dot(out.ml[at, :], out.mr[...], 1, 1), 2)
    arrive(rec.at[2], 2)
    unpack(2)

    def middle_tile(t):
        mid = finish(t, strided(t), xt[t], out)
        mt[t] = mid

    tiles(middle_tile)
    tiles(lambda t: project_left(t, mt[t], inc))
    send_staged(3)
    tiles(lambda t: project_right(t, inc))
    send_staged(4)
    tiles(lambda t: project_gate(t, inc))
    arrive(rec.at[3], 3)
    assemble(3, inc.ml)
    arrive(rec.at[4], 4)
    assemble(4, inc.mr)
    send_rows(lambda at: dot(inc.ml[:, at], inc.mr[...], 0, 0), 5)
    arrive(rec.at[5], 5)
    unpack(5)

    def result_tile(t):
        mt[t] = finish(t, strided(t), mt[t], inc)
        head_back(t, ct[t], inc)

    tiles(result_tile)
    send_staged(6)
    tiles(lambda t: out_tile(t, mt[t], res_v))
    res_out = pltpu.make_async_copy(res_v, res, osem.at[0])
    res_out.start()
    arrive(rec.at[6], 6)
    assemble(6, gmat)
    send_rows(lambda at: dot(inc.mr[at, :], gmat[...], 1, 1), 7)
    send_rows(lambda at: dot(inc.ml[at, :], gmat[...], 1, 0), 8)
    arrive(rec.at[7], 7)
    unpack(7)
    tiles(lambda t: pre_back_left(t, inc))
    arrive(rec.at[8], 8)
    unpack(8)
    tiles(lambda t: pre_back_right(t, inc))

    def grad_middle_tile(t):
        g = tail_back(t, ct[t], inc)
        gt[t] = g
        head_back(t, g, out)

    tiles(grad_middle_tile)
    send_staged(9)
    proj_grads(inc, GRD)
    rows_of_grads(4, GRD, dot(inc.nb[...], inc.gg[...], 1, 1))
    rows_of_grads(5, GRD, dot(inc.ub[...], inc.gl[...], 1, 1))
    rows_of_grads(6, GRD, dot(out.nb[...], out.gg[...], 1, 1))
    rows_of_grads(7, GRD, dot(out.ub[...], out.gl[...], 1, 1))
    pack_grads(ga[0], GRD)
    arrive(rec.at[9], 9)
    send_ready(ga[0], ga[1], 12)
    assemble(9, gmat)
    send_rows(lambda at: dot(gmat[at, :], out.mr[...], 1, 0), 10)
    send_rows(lambda at: dot(gmat[:, at], out.ml[...], 0, 0), 11)
    arrive(ga[1], 12)
    sum_grads(ga[1], ga[2], GRD)
    arrive(rec.at[10], 10)
    unpack(10)
    tiles(lambda t: pre_back_left(t, out))
    arrive(rec.at[11], 11)
    spread_grads(ga[2], 13)
    unpack(11)
    tiles(lambda t: pre_back_right(t, out))
    proj_grads(out, TAIL)
    pack_grads(gb[0], TAIL)
    send_ready(gb[0], gb[1], 14)
    tiles(lambda t: out_tile(t, tail_back(t, gt[t], out), grad_v))
    grad_out = pltpu.make_async_copy(grad_v, grad, osem.at[1])
    grad_out.start()
    arrive(gb[1], 14)
    sum_grads(gb[1], gb[2], TAIL)
    spread_grads(gb[2], 15)
    arrive(ga[2], 13)
    unpack_grads(ga[2], GRD)
    for j in range(4):
        write_rows(j, GRD, dpi.at[:, j * 128 : (j + 1) * 128])
    for j, dst in ((4, dgi), (5, dli), (6, dgo), (7, dlo)):
        write_rows(j, GRD, dst)
    arrive(gb[2], 15)
    unpack_grads(gb[2], TAIL)
    for j in range(4):
        write_rows(j, TAIL, dpo.at[:, j * 128 : (j + 1) * 128])

    for k in range(12):
        drain(snd.at[k], ssem, k)
    for g, k in ((ga, 12), (gb, 14)):
        drain(g[0], ssem, k)
        drain(g[2], ssem, k + 1)
    res_out.wait()
    grad_out.wait()


def scratch():
    shapes = []
    for _ in range(2):
        shapes += [pltpu.VMEM((TILES, 128, 128), F32)] * len(MODULE_FIELDS)
        shapes += [pltpu.VMEM((128, CELLS), BF16)] * len(FLAT_FIELDS)
        shapes += [
            pltpu.VMEM((512, CELLS), BF16),
            pltpu.VMEM((TILES, 8, 128), F32),
            pltpu.VMEM((TILES, 8, 128), F32),
            pltpu.VMEM((512, 128), BF16),
            pltpu.VMEM((128, 128), BF16),
            pltpu.VMEM((128, 128), BF16),
            pltpu.VMEM((WIDE, WIDE), BF16),
            pltpu.VMEM((WIDE, WIDE), BF16),
        ]
    shapes += [pltpu.VMEM((TILES, 128, 128), F32)] * 4
    shapes += [
        pltpu.VMEM((DEVICES * SGL, 128), F32),
        pltpu.VMEM((WIDE, WIDE), BF16),
        pltpu.VMEM((12, DEVICES, 3, 4, 128), BF16),
        pltpu.VMEM((12, DEVICES, 3, 4, 128), BF16),
        pltpu.VMEM((BI, BK, C), F32),
        pltpu.VMEM((BI, BK, C), F32),
        pltpu.VMEM((DEVICES * GRD, 128), F32),
    ]
    shapes += [pltpu.VMEM((DEVICES, GRD, 128), BF16)] * 3
    shapes += [pltpu.VMEM((DEVICES, TAIL, 128), BF16)] * 3
    shapes += [
        pltpu.SemaphoreType.DMA((16,)),
        pltpu.SemaphoreType.DMA((16,)),
        pltpu.SemaphoreType.DMA((2,)),
    ]
    return shapes


def publish(*refs):
    src, dst, held, sem_in, sem_out = refs[:8], refs[8:16], refs[16:24], refs[24], refs[25]
    ins = [pltpu.make_async_copy(src[j], held[j], sem_in.at[j]) for j in range(8)]
    outs = [pltpu.make_async_copy(held[j], dst[j], sem_out.at[j]) for j in range(8)]
    for copy in ins:
        copy.start()
    for copy_in, copy_out in zip(ins, outs):
        copy_in.wait()
        copy_out.start()
    for copy in outs:
        copy.wait()


def local(*args):
    vmem = pl.BlockSpec(memory_space=pltpu.VMEM)
    anywhere = pl.BlockSpec(memory_space=pl.ANY)
    pair = jax.ShapeDtypeStruct((BI, BK, C), F32)
    square = jax.ShapeDtypeStruct((C, C), F32)
    proj = jax.ShapeDtypeStruct((C, 4 * C), F32)
    shapes = (pair, pair, proj, square, square, proj, square, square)
    results = pl.pallas_call(
        kernel,
        out_shape=shapes,
        in_specs=[vmem] * 8,
        out_specs=(anywhere,) * 2 + (vmem,) * 6,
        scratch_shapes=scratch(),
        compiler_params=pltpu.CompilerParams(
            has_side_effects=True, collective_id=0, vmem_limit_bytes=58 * 2**20
        ),
        name="triangles",
    )(*args)
    return pl.pallas_call(
        publish,
        out_shape=shapes,
        in_specs=[anywhere] * 8,
        out_specs=(anywhere,) * 8,
        scratch_shapes=[pltpu.VMEM(v.shape, F32) for v in shapes] + [pltpu.SemaphoreType.DMA((8,))] * 2,
        name="publish",
    )(*results)


def solution(mesh):
    specs = (P("row", "col", None), P("row", "col", None), P(), P(), P(), P(), P(), P())
    return jax.shard_map(local, mesh=mesh, in_specs=specs, out_specs=specs, check_vma=False)
```

```python
import types

import jax
import jax.numpy as jnp
from jax import lax
from jax.experimental import pallas as pl
from jax.experimental.pallas import tpu as pltpu
from jax.sharding import PartitionSpec as P

F32 = jnp.float32
BF16 = jnp.bfloat16
EPSILON = 1e-05
MESH = pl.DeviceIdType.MESH

ROWS, COLS, DEVICES = 16, 8, 128
BI, BK, C = 24, 48, 128
TILES = 12
SLOT = 64
WIDE = COLS * SLOT
CELLS = TILES * 128
SGL = 16
GRD, TAIL = 8, 4
OFFSETS = sorted(
    ((dx, dy, dz, dc) for dx in range(4) for dy in range(4) for dz in range(4) for dc in range(2)),
    key=lambda o: -sum(min(v, 4 - v) for v in o[:3]),
)
OFFSETS.remove((0, 0, 0, 0))

MODULE_FIELDS = ("n", "s1", "p2", "s3", "p4", "gate", "u", "lifted")
FLAT_FIELDS = ("nb", "ub", "gl", "gg")


def dot(a, b, ca=1, cb=0):
    return lax.dot_general(a, b, (((ca,), (cb,)), ((), ())), preferred_element_type=F32)


def norm(p):
    d = p - jnp.mean(p, axis=0, keepdims=True)
    r = lax.rsqrt(jnp.mean(d * d, axis=0, keepdims=True) + EPSILON)
    return d * r, r


def norm_back(q, n, r):
    return (q - jnp.mean(q, axis=0, keepdims=True) - n * jnp.mean(q * n, axis=0, keepdims=True)) * r


def lanes(t):
    return pl.ds(pl.multiple_of(t * 128, 128), 128)


def kernel(*refs):
    sources, results, taken, isem = refs[:8], refs[8:16], refs[16:24], refs[24]
    pair, cot, wp_o, wg_o, wl_o, wp_i, wg_i, wl_i = taken
    it = iter(refs[25:])

    def enter(j):
        return pltpu.make_async_copy(sources[j], taken[j], isem.at[j])

    for j in (0, 2, 3, 4, 5, 6, 7, 1):
        enter(j).start()

    def module(wp, wg, wl):
        m = types.SimpleNamespace(wp=wp, wg=wg, wl=wl)
        for name in MODULE_FIELDS + FLAT_FIELDS + ("gp", "r", "ur", "wpt", "wgt", "wlt", "ml", "mr"):
            setattr(m, name, next(it))
        return m

    out, inc = module(wp_o, wg_o, wl_o), module(wp_i, wg_i, wl_i)
    xt, ct, mt, gt, stage, gmat, snd, rec, pg = (next(it) for _ in range(9))
    ws, ga, gb, ssem, rsem = next(it), (next(it), next(it), next(it)), (next(it), next(it), next(it)), next(it), next(it)
    osem = next(it)
    held = tuple(it)
    res, grad, dpo, dgo, dlo, dpi, dgi, dli = held

    row, col = lax.axis_index("row"), lax.axis_index("col")
    me = row * COLS + col
    x = row // 8 * 2 + lax.rem(col, 2)
    xs = [lax.rem(x + d, 4) for d in range(4)]
    row_x = [v // 2 * 8 for v in xs]
    col_x = [lax.rem(v, 2) for v in xs]
    row_z = [lax.rem(lax.rem(row, 8) // 2 + d, 4) * 2 for d in range(4)]
    col_y = [lax.rem(col // 2 + d, 4) * 2 for d in range(4)]
    row_c = [lax.rem(row + d, 2) for d in range(2)]

    def peers(visit):
        for dx, dy, dz, dc in OFFSETS:
            visit(row_x[dx] + row_z[dz] + row_c[dc], col_y[dy] + col_x[dx])

    barrier = pltpu.get_barrier_semaphore()
    peers(lambda rr, cc: pl.semaphore_signal(barrier, inc=1, device_id=(rr, cc), device_id_type=MESH))

    def start(src, dst, k, rr, cc):
        pltpu.make_async_remote_copy(
            src, dst, ssem.at[k], rsem.at[k], device_id=(rr, cc), device_id_type=MESH
        ).start()

    def drain(ref, sem, k):
        span = ref.at[pl.ds(0, DEVICES - 1)]
        pltpu.make_async_copy(span, span, sem.at[k]).wait()

    def leave(j):
        return pltpu.make_async_copy(held[j], results[j], osem.at[j])

    def arrive(ref, k):
        drain(ref, rsem, k)

    def piece(p):
        return stage[pl.ds(pl.multiple_of(p * SGL, SGL), SGL), :]

    def put(ref, p, value):
        for j in range(3):
            ref[p, j] = value[4 * j : 4 * j + 4].astype(BF16)

    def send_staged(k):
        def visit(rr, cc):
            p = rr * COLS + cc
            put(snd.at[k], p, piece(p))
            start(snd.at[k, p], rec.at[k, me], k, rr, cc)

        peers(visit)
        put(rec.at[k], me, piece(me))

    def send_ready(src, dst, k):
        peers(lambda rr, cc: start(src.at[rr * COLS + cc], dst.at[me], k, rr, cc))
        dst[me] = src[me]

    def unpack(k):
        def step(a, carry):
            for b in range(COLS):
                p = a * COLS + b
                for j in range(3):
                    stage[pl.ds(pl.multiple_of(p * SGL, SGL) + 4 * j, 4), :] = rec[k, p, j].astype(F32)
            return carry

        lax.fori_loop(0, ROWS, step, 0)

    def tiles(body):
        lax.fori_loop(0, TILES, lambda t, carry: (body(t), carry)[1], 0, unroll=4)

    low = lax.broadcasted_iota(jnp.int32, (BI, 128), 1) < SLOT
    top = lax.broadcasted_iota(jnp.int32, (BI, 128), 0) < TILES
    gap8 = jnp.zeros((8, 128), F32)
    gap16 = jnp.zeros((16, 128), F32)

    def swap_lanes(a):
        return pltpu.roll(a, SLOT, 1)

    def swap_rows(a):
        return pltpu.roll(a, TILES, 0)

    def halves(a, b):
        return jnp.where(low, a, swap_lanes(b)), jnp.where(low, swap_lanes(a), b)

    def assemble(k, whole):
        unpack(k)

        def step(r2, carry):
            at = pl.ds(pl.multiple_of(r2 * SLOT, SLOT), SLOT)
            for m in range(COLS // 2):
                ls = []
                for s in range(2):
                    p = (2 * r2 + s) * COLS + 2 * m
                    a, b = (jnp.concatenate([piece(q), gap8], axis=0) for q in (p, p + 1))
                    o0, o1 = halves(a, b)
                    ls.append(jnp.where(top, o0, swap_rows(o1)))
                whole[at, m * 128 : (m + 1) * 128] = jnp.concatenate(ls + [gap16], axis=0).astype(BF16)
            return carry

        lax.fori_loop(0, ROWS // 2, step, 0)

    half = row // 4

    def send_rows(rows_of, k):
        def step(i, carry):
            q = lax.rem(half // 2 + 1 + i // 2, 2) * 2 + lax.rem(half + 1 + i, 2)
            block = rows_of(pl.ds(pl.multiple_of(q * 128, 128), 128))
            for s4 in range(4):
                lo = SLOT * (s4 // 2) + BI * (s4 % 2)
                for m in range(COLS // 2):
                    p = (4 * q + s4) * COLS + 2 * m
                    first = block[lo : lo + BI, m * 128 : (m + 1) * 128]
                    a, b = halves(first, swap_rows(first))
                    put(snd.at[k], p, a)
                    put(snd.at[k], p + 1, b)
            for d in (2, 1, 3, 0):
                for s4 in range(4):
                    for x_lo in range(2):
                        rr, cc = 4 * q + s4, col_y[d] + x_lo
                        p = rr * COLS + cc
                        if d:
                            start(snd.at[k, p], rec.at[k, me], k, rr, cc)
                        else:
                            @pl.when(p != me)
                            def _():
                                start(snd.at[k, p], rec.at[k, me], k, rr, cc)
            return carry

        lax.fori_loop(0, WIDE // 128, step, 0)
        rec[k, me] = snd[k, me]

    def into_tiles(src, dst):
        def body(t):
            rows = jnp.concatenate([src[t], gap16, src[TILES + t], gap16], axis=0)
            dst[t] = rows.T

        tiles(body)

    def out_tile(t, value, dst):
        back = value.T
        dst[t] = back[:BK]
        dst[TILES + t] = back[SLOT : SLOT + BK]

    def strided(t):
        return stage[pl.ds(t, 128, stride=SGL), :]

    def put_strided(t, value):
        stage[pl.ds(t, 128, stride=SGL), :] = value

    def project_left(t, x, m):
        n, r = norm(x)
        nb = n.astype(BF16)
        m.n[t] = n
        m.r[t] = jnp.broadcast_to(r, (8, 128))
        m.nb[:, lanes(t)] = nb
        s1 = jax.nn.sigmoid(dot(m.wpt[0:128], nb))
        p2 = dot(m.wpt[128:256], nb)
        m.s1[t] = s1
        m.p2[t] = p2
        put_strided(t, s1 * p2)

    def project_right(t, m):
        nb = m.nb[:, lanes(t)]
        s3 = jax.nn.sigmoid(dot(m.wpt[256:384], nb))
        p4 = dot(m.wpt[384:512], nb)
        m.s3[t] = s3
        m.p4[t] = p4
        put_strided(t, s3 * p4)

    def project_gate(t, m):
        m.gate[t] = jax.nn.sigmoid(dot(m.wgt[...], m.nb[:, lanes(t)]))

    def finish(t, tri, base, m):
        u, r = norm(tri)
        ub = u.astype(BF16)
        m.u[t] = u
        m.ur[t] = jnp.broadcast_to(r, (8, 128))
        m.ub[:, lanes(t)] = ub
        lifted = dot(m.wlt[...], ub)
        m.lifted[t] = lifted
        return base + m.gate[t] * lifted

    def head_back(t, g, m):
        gate = m.gate[t]
        through = g * gate
        gl = through.astype(BF16)
        m.gl[:, lanes(t)] = gl
        m.gg[:, lanes(t)] = (through * m.lifted[t] * (1.0 - gate)).astype(BF16)
        gunit = dot(m.wl[...], gl)
        put_strided(t, norm_back(gunit, m.u[t], m.ur[t][0:1]))

    def pre_back_left(t, m):
        s1 = m.s1[t]
        a = strided(t) * s1
        m.gp[0:128, lanes(t)] = (a * m.p2[t] * (1.0 - s1)).astype(BF16)
        m.gp[128:256, lanes(t)] = a.astype(BF16)
        pg[t] = dot(m.wp[:, 0:256], m.gp[0:256, lanes(t)]) + dot(m.wg[...], m.gg[:, lanes(t)])

    def pre_back_right(t, m):
        s3 = m.s3[t]
        b = strided(t) * s3
        m.gp[256:384, lanes(t)] = (b * m.p4[t] * (1.0 - s3)).astype(BF16)
        m.gp[384:512, lanes(t)] = b.astype(BF16)

    def tail_back(t, g, m):
        gn = pg[t] + dot(m.wp[:, 256:512], m.gp[256:512, lanes(t)])
        return g + norm_back(gn, m.n[t], m.r[t][0:1])

    def rows_of_grads(j, size, value):
        ws[pl.ds(j, 128, stride=size), :] = value

    def proj_grads(m, size, columns):
        for j in columns:
            rows_of_grads(j, size, dot(m.nb[...], m.gp[j * 128 : (j + 1) * 128, :], 1, 1))

    def pack_grads(snd, size):
        def step(a, carry):
            for b in range(COLS):
                at = pl.multiple_of(a * (COLS * size), 8) + b * size
                snd[a * COLS + b] = ws[pl.ds(at, size), :].astype(BF16)
            return carry

        lax.fori_loop(0, ROWS, step, 0)

    def sum_grads(rec, whole, size):
        whole[me] = lax.fori_loop(
            0,
            ROWS,
            lambda a, acc: acc + jnp.sum(rec[pl.ds(a * COLS, COLS)].astype(F32), axis=0),
            jnp.zeros((size, 128), F32),
        ).astype(BF16)

    def spread_grads(whole, k):
        peers(lambda rr, cc: start(whole.at[me], whole.at[me], k, rr, cc))

    def unpack_grads(whole, size):
        def step(a, carry):
            for b in range(COLS):
                at = pl.multiple_of(a * (COLS * size), 8) + b * size
                ws[pl.ds(at, size), :] = whole[a * COLS + b].astype(F32)
            return carry

        lax.fori_loop(0, ROWS, step, 0)

    def write_rows(j, size, dst):
        dst[...] = ws[pl.ds(j, 128, stride=size), :]

    def turn(m, first):
        for j in range(first, first + 3):
            enter(j).wait()
        m.wpt[...] = m.wp[...].T
        m.wgt[...] = m.wg[...].T
        m.wlt[...] = m.wl[...].T

    enter(0).wait()
    into_tiles(pair, xt)
    turn(out, 2)
    tiles(lambda t: project_left(t, xt[t], out))
    pl.semaphore_wait(barrier, DEVICES - 1)
    send_staged(0)
    tiles(lambda t: project_right(t, out))
    send_staged(1)
    tiles(lambda t: project_gate(t, out))
    enter(1).wait()
    into_tiles(cot, ct)
    turn(inc, 5)
    arrive(rec.at[0], 0)
    assemble(0, out.ml)
    arrive(rec.at[1], 1)
    assemble(1, out.mr)
    send_rows(lambda at: dot(out.ml[at, :], out.mr[...], 1, 1), 2)
    arrive(rec.at[2], 2)
    unpack(2)

    def middle_tile(t):
        mid = finish(t, strided(t), xt[t], out)
        mt[t] = mid

    tiles(middle_tile)
    tiles(lambda t: project_left(t, mt[t], inc))
    send_staged(3)
    tiles(lambda t: project_right(t, inc))
    send_staged(4)
    tiles(lambda t: project_gate(t, inc))
    arrive(rec.at[3], 3)
    assemble(3, inc.ml)
    arrive(rec.at[4], 4)
    assemble(4, inc.mr)
    send_rows(lambda at: dot(inc.ml[:, at], inc.mr[...], 0, 0), 5)
    arrive(rec.at[5], 5)
    unpack(5)

    def result_tile(t):
        mt[t] = finish(t, strided(t), mt[t], inc)
        head_back(t, ct[t], inc)

    tiles(result_tile)
    send_staged(6)
    tiles(lambda t: out_tile(t, mt[t], res))
    leave(0).start()
    arrive(rec.at[6], 6)
    assemble(6, gmat)
    send_rows(lambda at: dot(inc.mr[at, :], gmat[...], 1, 1), 7)
    send_rows(lambda at: dot(inc.ml[at, :], gmat[...], 1, 0), 8)
    arrive(rec.at[7], 7)
    unpack(7)
    tiles(lambda t: pre_back_left(t, inc))
    arrive(rec.at[8], 8)
    unpack(8)

    def grad_middle_tile(t):
        pre_back_right(t, inc)
        g = tail_back(t, ct[t], inc)
        gt[t] = g
        head_back(t, g, out)

    tiles(grad_middle_tile)
    send_staged(9)
    proj_grads(inc, GRD, range(4))
    rows_of_grads(4, GRD, dot(inc.nb[...], inc.gg[...], 1, 1))
    rows_of_grads(5, GRD, dot(inc.ub[...], inc.gl[...], 1, 1))
    rows_of_grads(6, GRD, dot(out.nb[...], out.gg[...], 1, 1))
    rows_of_grads(7, GRD, dot(out.ub[...], out.gl[...], 1, 1))
    pack_grads(ga[0], GRD)
    arrive(rec.at[9], 9)
    assemble(9, gmat)
    send_rows(lambda at: dot(gmat[at, :], out.mr[...], 1, 0), 10)
    send_rows(lambda at: dot(gmat[:, at], out.ml[...], 0, 0), 11)
    send_ready(ga[0], ga[1], 12)
    arrive(rec.at[10], 10)
    unpack(10)
    tiles(lambda t: pre_back_left(t, out))
    proj_grads(out, TAIL, (0, 1))
    arrive(rec.at[11], 11)
    unpack(11)
    tiles(lambda t: pre_back_right(t, out))
    proj_grads(out, TAIL, (2, 3))
    pack_grads(gb[0], TAIL)
    send_ready(gb[0], gb[1], 14)
    arrive(ga[1], 12)
    sum_grads(ga[1], ga[2], GRD)
    spread_grads(ga[2], 13)
    tiles(lambda t: out_tile(t, tail_back(t, gt[t], out), grad))
    leave(1).start()
    arrive(gb[1], 14)
    sum_grads(gb[1], gb[2], TAIL)
    spread_grads(gb[2], 15)
    arrive(ga[2], 13)
    unpack_grads(ga[2], GRD)
    for j in range(4):
        write_rows(j, GRD, dpi.at[:, j * 128 : (j + 1) * 128])
    for j, dst in ((4, dgi), (5, dli), (6, dgo), (7, dlo)):
        write_rows(j, GRD, dst)
    for j in range(3, 8):
        leave(j).start()
    arrive(gb[2], 15)
    unpack_grads(gb[2], TAIL)
    for j in range(4):
        write_rows(j, TAIL, dpo.at[:, j * 128 : (j + 1) * 128])
    leave(2).start()

    for k in range(12):
        drain(snd.at[k], ssem, k)
    for g, k in ((ga, 12), (gb, 14)):
        drain(g[0], ssem, k)
        drain(g[2], ssem, k + 1)
    for j in range(8):
        leave(j).wait()


def scratch(arguments, results):
    shapes = [pltpu.VMEM(v.shape, v.dtype) for v in arguments] + [pltpu.SemaphoreType.DMA((8,))]
    for _ in range(2):
        shapes += [pltpu.VMEM((TILES, 128, 128), F32)] * len(MODULE_FIELDS)
        shapes += [pltpu.VMEM((128, CELLS), BF16)] * len(FLAT_FIELDS)
        shapes += [
            pltpu.VMEM((512, CELLS), BF16),
            pltpu.VMEM((TILES, 8, 128), F32),
            pltpu.VMEM((TILES, 8, 128), F32),
            pltpu.VMEM((512, 128), BF16),
            pltpu.VMEM((128, 128), BF16),
            pltpu.VMEM((128, 128), BF16),
            pltpu.VMEM((WIDE, WIDE), BF16),
            pltpu.VMEM((WIDE, WIDE), BF16),
        ]
    shapes += [pltpu.VMEM((TILES, 128, 128), F32)] * 4
    shapes += [
        pltpu.VMEM((DEVICES * SGL, 128), F32),
        pltpu.VMEM((WIDE, WIDE), BF16),
        pltpu.VMEM((12, DEVICES, 3, 4, 128), BF16),
        pltpu.VMEM((12, DEVICES, 3, 4, 128), BF16),
        pltpu.VMEM((TILES, 128, 128), F32),
        pltpu.VMEM((DEVICES * GRD, 128), F32),
    ]
    shapes += [pltpu.VMEM((DEVICES, GRD, 128), BF16)] * 3
    shapes += [pltpu.VMEM((DEVICES, TAIL, 128), BF16)] * 3
    shapes += [
        pltpu.SemaphoreType.DMA((16,)),
        pltpu.SemaphoreType.DMA((16,)),
        pltpu.SemaphoreType.DMA((8,)),
    ]
    return shapes + [pltpu.VMEM(v.shape, F32) for v in results]


def publish(*refs):
    src, dst, held, sem_in, sem_out = refs[:8], refs[8:16], refs[16:24], refs[24], refs[25]
    ins = [pltpu.make_async_copy(src[j], held[j], sem_in.at[j]) for j in range(8)]
    outs = [pltpu.make_async_copy(held[j], dst[j], sem_out.at[j]) for j in range(8)]
    for copy in ins:
        copy.start()
    for copy_in, copy_out in zip(ins, outs):
        copy_in.wait()
        copy_out.start()
    for copy in outs:
        copy.wait()


def local(*args):
    anywhere = pl.BlockSpec(memory_space=pl.ANY)
    pair = jax.ShapeDtypeStruct((BI, BK, C), F32)
    square = jax.ShapeDtypeStruct((C, C), F32)
    proj = jax.ShapeDtypeStruct((C, 4 * C), F32)
    shapes = (pair, pair, proj, square, square, proj, square, square)
    results = pl.pallas_call(
        kernel,
        out_shape=shapes,
        in_specs=[anywhere] * 8,
        out_specs=(anywhere,) * 8,
        scratch_shapes=scratch(args, shapes),
        compiler_params=pltpu.CompilerParams(
            has_side_effects=True, collective_id=0, vmem_limit_bytes=58 * 2**20
        ),
        name="triangles",
    )(*args)
    return pl.pallas_call(
        publish,
        out_shape=shapes,
        in_specs=[anywhere] * 8,
        out_specs=(anywhere,) * 8,
        scratch_shapes=[pltpu.VMEM(v.shape, F32) for v in shapes] + [pltpu.SemaphoreType.DMA((8,))] * 2,
        name="publish",
    )(*results)


def solution(mesh):
    specs = (P("row", "col", None), P("row", "col", None), P(), P(), P(), P(), P(), P())
    return jax.shard_map(local, mesh=mesh, in_specs=specs, out_specs=specs, check_vma=False)
```

```python
import types

import jax
import jax.numpy as jnp
from jax import lax
from jax.experimental import pallas as pl
from jax.experimental.pallas import tpu as pltpu
from jax.sharding import PartitionSpec as P

F32 = jnp.float32
BF16 = jnp.bfloat16
EPSILON = 1e-05
MESH = pl.DeviceIdType.MESH

ROWS, COLS, DEVICES = 16, 8, 128
BI, BK, C = 24, 48, 128
TILES = 12
SLOT = 64
WIDE = COLS * SLOT
CELLS = TILES * 128
SGL = 16
GRD, TAIL = 8, 4
OFFSETS = sorted(
    ((dx, dy, dz, dc) for dx in range(4) for dy in range(4) for dz in range(4) for dc in range(2)),
    key=lambda o: -sum(min(v, 4 - v) for v in o[:3]),
)
OFFSETS.remove((0, 0, 0, 0))

MODULE_FIELDS = ("n", "s1", "p2", "s3", "p4", "gate", "u", "lifted")
FLAT_FIELDS = ("nb", "ub", "gl", "gg")


def dot(a, b, ca=1, cb=0):
    return lax.dot_general(a, b, (((ca,), (cb,)), ((), ())), preferred_element_type=F32)


def norm(p):
    d = p - jnp.mean(p, axis=0, keepdims=True)
    r = lax.rsqrt(jnp.mean(d * d, axis=0, keepdims=True) + EPSILON)
    return d * r, r


def norm_back(q, n, r):
    return (q - jnp.mean(q, axis=0, keepdims=True) - n * jnp.mean(q * n, axis=0, keepdims=True)) * r


def lanes(t):
    return pl.ds(pl.multiple_of(t * 128, 128), 128)


def kernel(*refs):
    sources, results, taken, isem = refs[:8], refs[8:16], refs[16:24], refs[24]
    pair, cot, wp_o, wg_o, wl_o, wp_i, wg_i, wl_i = taken
    it = iter(refs[25:])

    def enter(j):
        return pltpu.make_async_copy(sources[j], taken[j], isem.at[j])

    for j in (0, 2, 3, 4, 5, 6, 7, 1):
        enter(j).start()

    def module(wp, wg, wl):
        m = types.SimpleNamespace(wp=wp, wg=wg, wl=wl)
        for name in MODULE_FIELDS + FLAT_FIELDS + ("gp", "r", "ur", "wpt", "wgt", "wlt", "ml", "mr"):
            setattr(m, name, next(it))
        return m

    out, inc = module(wp_o, wg_o, wl_o), module(wp_i, wg_i, wl_i)
    xt, ct, mt, gt, stage, gmat, snd, rec, pg = (next(it) for _ in range(9))
    ws, ga, gb, ssem, rsem = next(it), (next(it), next(it), next(it)), (next(it), next(it), next(it)), next(it), next(it)
    osem = next(it)
    held = tuple(it)
    res, grad, dpo, dgo, dlo, dpi, dgi, dli = held

    row, col = lax.axis_index("row"), lax.axis_index("col")
    me = row * COLS + col
    x = row // 8 * 2 + lax.rem(col, 2)
    xs = [lax.rem(x + d, 4) for d in range(4)]
    row_x = [v // 2 * 8 for v in xs]
    col_x = [lax.rem(v, 2) for v in xs]
    row_z = [lax.rem(lax.rem(row, 8) // 2 + d, 4) * 2 for d in range(4)]
    col_y = [lax.rem(col // 2 + d, 4) * 2 for d in range(4)]
    row_c = [lax.rem(row + d, 2) for d in range(2)]

    def peers(visit):
        for dx, dy, dz, dc in OFFSETS:
            visit(row_x[dx] + row_z[dz] + row_c[dc], col_y[dy] + col_x[dx])

    barrier = pltpu.get_barrier_semaphore()
    peers(lambda rr, cc: pl.semaphore_signal(barrier, inc=1, device_id=(rr, cc), device_id_type=MESH))

    def start(src, dst, k, rr, cc):
        pltpu.make_async_remote_copy(
            src, dst, ssem.at[k], rsem.at[k], device_id=(rr, cc), device_id_type=MESH
        ).start()

    def drain(ref, sem, k):
        span = ref.at[pl.ds(0, DEVICES - 1)]
        pltpu.make_async_copy(span, span, sem.at[k]).wait()

    def leave(j):
        return pltpu.make_async_copy(held[j], results[j], osem.at[j])

    def arrive(ref, k):
        drain(ref, rsem, k)

    def piece(p):
        return stage[pl.ds(pl.multiple_of(p * SGL, SGL), SGL), :]

    def put(ref, p, value):
        for j in range(3):
            ref[p, j] = value[4 * j : 4 * j + 4].astype(BF16)

    def send_staged(k):
        def visit(rr, cc):
            p = rr * COLS + cc
            put(snd.at[k], p, piece(p))
            start(snd.at[k, p], rec.at[k, me], k, rr, cc)

        peers(visit)
        put(rec.at[k], me, piece(me))

    def send_ready(src, dst, k):
        peers(lambda rr, cc: start(src.at[rr * COLS + cc], dst.at[me], k, rr, cc))
        dst[me] = src[me]

    def unpack(k):
        def step(a, carry):
            for b in range(COLS):
                p = a * COLS + b
                for j in range(3):
                    stage[pl.ds(pl.multiple_of(p * SGL, SGL) + 4 * j, 4), :] = rec[k, p, j].astype(F32)
            return carry

        lax.fori_loop(0, ROWS, step, 0)

    def tiles(body):
        lax.fori_loop(0, TILES, lambda t, carry: (body(t), carry)[1], 0, unroll=6)

    low = lax.broadcasted_iota(jnp.int32, (BI, 128), 1) < SLOT
    top = lax.broadcasted_iota(jnp.int32, (BI, 128), 0) < TILES
    gap8 = jnp.zeros((8, 128), F32)
    gap16 = jnp.zeros((16, 128), F32)

    def swap_lanes(a):
        return pltpu.roll(a, SLOT, 1)

    def swap_rows(a):
        return pltpu.roll(a, TILES, 0)

    def halves(a, b):
        return jnp.where(low, a, swap_lanes(b)), jnp.where(low, swap_lanes(a), b)

    def assemble(k, whole):
        unpack(k)

        def step(r2, carry):
            at = pl.ds(pl.multiple_of(r2 * SLOT, SLOT), SLOT)
            for m in range(COLS // 2):
                ls = []
                for s in range(2):
                    p = (2 * r2 + s) * COLS + 2 * m
                    a, b = (jnp.concatenate([piece(q), gap8], axis=0) for q in (p, p + 1))
                    o0, o1 = halves(a, b)
                    ls.append(jnp.where(top, o0, swap_rows(o1)))
                whole[at, m * 128 : (m + 1) * 128] = jnp.concatenate(ls + [gap16], axis=0).astype(BF16)
            return carry

        lax.fori_loop(0, ROWS // 2, step, 0)

    half = row // 4

    def send_rows(rows_of, k):
        def step(i, carry):
            q = lax.rem(half // 2 + 1 + i // 2, 2) * 2 + lax.rem(half + 1 + i, 2)
            block = rows_of(pl.ds(pl.multiple_of(q * 128, 128), 128))
            for s4 in range(4):
                lo = SLOT * (s4 // 2) + BI * (s4 % 2)
                for m in range(COLS // 2):
                    p = (4 * q + s4) * COLS + 2 * m
                    first = block[lo : lo + BI, m * 128 : (m + 1) * 128]
                    a, b = halves(first, swap_rows(first))
                    put(snd.at[k], p, a)
                    put(snd.at[k], p + 1, b)
            for d in (2, 1, 3, 0):
                for s4 in range(4):
                    for x_lo in range(2):
                        rr, cc = 4 * q + s4, col_y[d] + x_lo
                        p = rr * COLS + cc
                        if d:
                            start(snd.at[k, p], rec.at[k, me], k, rr, cc)
                        else:
                            @pl.when(p != me)
                            def _():
                                start(snd.at[k, p], rec.at[k, me], k, rr, cc)
            return carry

        lax.fori_loop(0, WIDE // 128, step, 0)
        rec[k, me] = snd[k, me]

    def into_tiles(src, dst):
        def body(t):
            rows = jnp.concatenate([src[t], gap16, src[TILES + t], gap16], axis=0)
            dst[t] = rows.T

        tiles(body)

    def out_tile(t, value, dst):
        back = value.T
        dst[t] = back[:BK]
        dst[TILES + t] = back[SLOT : SLOT + BK]

    def strided(t):
        return stage[pl.ds(t, 128, stride=SGL), :]

    def put_strided(t, value):
        stage[pl.ds(t, 128, stride=SGL), :] = value

    def project_left(t, x, m):
        n, r = norm(x)
        nb = n.astype(BF16)
        m.n[t] = n
        m.r[t] = jnp.broadcast_to(r, (8, 128))
        m.nb[:, lanes(t)] = nb
        s1 = jax.nn.sigmoid(dot(m.wpt[0:128], nb))
        p2 = dot(m.wpt[128:256], nb)
        m.s1[t] = s1
        m.p2[t] = p2
        put_strided(t, s1 * p2)

    def project_right(t, m):
        nb = m.nb[:, lanes(t)]
        s3 = jax.nn.sigmoid(dot(m.wpt[256:384], nb))
        p4 = dot(m.wpt[384:512], nb)
        m.s3[t] = s3
        m.p4[t] = p4
        put_strided(t, s3 * p4)

    def project_gate(t, m):
        m.gate[t] = jax.nn.sigmoid(dot(m.wgt[...], m.nb[:, lanes(t)]))

    def finish(t, tri, base, m):
        u, r = norm(tri)
        ub = u.astype(BF16)
        m.u[t] = u
        m.ur[t] = jnp.broadcast_to(r, (8, 128))
        m.ub[:, lanes(t)] = ub
        lifted = dot(m.wlt[...], ub)
        m.lifted[t] = lifted
        return base + m.gate[t] * lifted

    def head_back(t, g, m):
        gate = m.gate[t]
        through = g * gate
        gl = through.astype(BF16)
        m.gl[:, lanes(t)] = gl
        m.gg[:, lanes(t)] = (through * m.lifted[t] * (1.0 - gate)).astype(BF16)
        gunit = dot(m.wl[...], gl)
        put_strided(t, norm_back(gunit, m.u[t], m.ur[t][0:1]))

    def pre_back_left(t, m):
        s1 = m.s1[t]
        a = strided(t) * s1
        m.gp[0:128, lanes(t)] = (a * m.p2[t] * (1.0 - s1)).astype(BF16)
        m.gp[128:256, lanes(t)] = a.astype(BF16)
        pg[t] = dot(m.wp[:, 0:256], m.gp[0:256, lanes(t)]) + dot(m.wg[...], m.gg[:, lanes(t)])

    def pre_back_right(t, m):
        s3 = m.s3[t]
        b = strided(t) * s3
        m.gp[256:384, lanes(t)] = (b * m.p4[t] * (1.0 - s3)).astype(BF16)
        m.gp[384:512, lanes(t)] = b.astype(BF16)

    def tail_back(t, g, m):
        gn = pg[t] + dot(m.wp[:, 256:512], m.gp[256:512, lanes(t)])
        return g + norm_back(gn, m.n[t], m.r[t][0:1])

    def rows_of_grads(j, size, value):
        ws[pl.ds(j, 128, stride=size), :] = value

    def proj_grads(m, size, columns):
        for j in columns:
            rows_of_grads(j, size, dot(m.nb[...], m.gp[j * 128 : (j + 1) * 128, :], 1, 1))

    def pack_grads(snd, size):
        def step(a, carry):
            for b in range(COLS):
                at = pl.multiple_of(a * (COLS * size), 8) + b * size
                snd[a * COLS + b] = ws[pl.ds(at, size), :].astype(BF16)
            return carry

        lax.fori_loop(0, ROWS, step, 0)

    def sum_grads(rec, whole, size):
        whole[me] = lax.fori_loop(
            0,
            ROWS,
            lambda a, acc: acc + jnp.sum(rec[pl.ds(a * COLS, COLS)].astype(F32), axis=0),
            jnp.zeros((size, 128), F32),
        ).astype(BF16)

    def spread_grads(whole, k):
        peers(lambda rr, cc: start(whole.at[me], whole.at[me], k, rr, cc))

    def unpack_grads(whole, size):
        def step(a, carry):
            for b in range(COLS):
                at = pl.multiple_of(a * (COLS * size), 8) + b * size
                ws[pl.ds(at, size), :] = whole[a * COLS + b].astype(F32)
            return carry

        lax.fori_loop(0, ROWS, step, 0)

    def write_rows(j, size, dst):
        dst[...] = ws[pl.ds(j, 128, stride=size), :]

    def turn(m, first):
        for j in range(first, first + 3):
            enter(j).wait()
        m.wpt[...] = m.wp[...].T
        m.wgt[...] = m.wg[...].T
        m.wlt[...] = m.wl[...].T

    enter(0).wait()
    into_tiles(pair, xt)
    turn(out, 2)
    tiles(lambda t: project_left(t, xt[t], out))
    pl.semaphore_wait(barrier, DEVICES - 1)
    send_staged(0)
    tiles(lambda t: project_right(t, out))
    send_staged(1)
    tiles(lambda t: project_gate(t, out))
    enter(1).wait()
    into_tiles(cot, ct)
    turn(inc, 5)
    arrive(rec.at[0], 0)
    assemble(0, out.ml)
    arrive(rec.at[1], 1)
    assemble(1, out.mr)
    send_rows(lambda at: dot(out.ml[at, :], out.mr[...], 1, 1), 2)
    arrive(rec.at[2], 2)
    unpack(2)

    def middle_tile(t):
        mid = finish(t, strided(t), xt[t], out)
        mt[t] = mid

    tiles(middle_tile)
    tiles(lambda t: project_left(t, mt[t], inc))
    send_staged(3)
    tiles(lambda t: project_right(t, inc))
    send_staged(4)
    tiles(lambda t: project_gate(t, inc))
    arrive(rec.at[3], 3)
    assemble(3, inc.ml)
    arrive(rec.at[4], 4)
    assemble(4, inc.mr)
    send_rows(lambda at: dot(inc.ml[:, at], inc.mr[...], 0, 0), 5)
    arrive(rec.at[5], 5)
    unpack(5)

    def result_tile(t):
        mt[t] = finish(t, strided(t), mt[t], inc)
        head_back(t, ct[t], inc)

    tiles(result_tile)
    send_staged(6)
    tiles(lambda t: out_tile(t, mt[t], res))
    leave(0).start()
    arrive(rec.at[6], 6)
    assemble(6, gmat)
    send_rows(lambda at: dot(inc.mr[at, :], gmat[...], 1, 1), 7)
    send_rows(lambda at: dot(inc.ml[at, :], gmat[...], 1, 0), 8)
    arrive(rec.at[7], 7)
    unpack(7)
    tiles(lambda t: pre_back_left(t, inc))
    arrive(rec.at[8], 8)
    unpack(8)

    def grad_middle_tile(t):
        gt[t] = tail_back(t, ct[t], inc)

    tiles(lambda t: pre_back_right(t, inc))
    tiles(grad_middle_tile)
    tiles(lambda t: head_back(t, gt[t], out))
    send_staged(9)
    proj_grads(inc, GRD, range(4))
    rows_of_grads(4, GRD, dot(inc.nb[...], inc.gg[...], 1, 1))
    rows_of_grads(5, GRD, dot(inc.ub[...], inc.gl[...], 1, 1))
    rows_of_grads(6, GRD, dot(out.nb[...], out.gg[...], 1, 1))
    rows_of_grads(7, GRD, dot(out.ub[...], out.gl[...], 1, 1))
    pack_grads(ga[0], GRD)
    arrive(rec.at[9], 9)
    assemble(9, gmat)
    send_rows(lambda at: dot(gmat[at, :], out.mr[...], 1, 0), 10)
    send_rows(lambda at: dot(gmat[:, at], out.ml[...], 0, 0), 11)
    send_ready(ga[0], ga[1], 12)
    arrive(rec.at[10], 10)
    unpack(10)
    tiles(lambda t: pre_back_left(t, out))
    proj_grads(out, TAIL, (0, 1))
    arrive(rec.at[11], 11)
    unpack(11)
    tiles(lambda t: pre_back_right(t, out))
    proj_grads(out, TAIL, (2, 3))
    pack_grads(gb[0], TAIL)
    send_ready(gb[0], gb[1], 14)
    arrive(ga[1], 12)
    sum_grads(ga[1], ga[2], GRD)
    spread_grads(ga[2], 13)
    tiles(lambda t: out_tile(t, tail_back(t, gt[t], out), grad))
    leave(1).start()
    arrive(gb[1], 14)
    sum_grads(gb[1], gb[2], TAIL)
    spread_grads(gb[2], 15)
    arrive(ga[2], 13)
    unpack_grads(ga[2], GRD)
    for j in range(4):
        write_rows(j, GRD, dpi.at[:, j * 128 : (j + 1) * 128])
    for j, dst in ((4, dgi), (5, dli), (6, dgo), (7, dlo)):
        write_rows(j, GRD, dst)
    for j in range(3, 8):
        leave(j).start()
    arrive(gb[2], 15)
    unpack_grads(gb[2], TAIL)
    for j in range(4):
        write_rows(j, TAIL, dpo.at[:, j * 128 : (j + 1) * 128])
    leave(2).start()

    for k in range(12):
        drain(snd.at[k], ssem, k)
    for g, k in ((ga, 12), (gb, 14)):
        drain(g[0], ssem, k)
        drain(g[2], ssem, k + 1)
    for j in range(8):
        leave(j).wait()


def scratch(arguments, results):
    shapes = [pltpu.VMEM(v.shape, v.dtype) for v in arguments] + [pltpu.SemaphoreType.DMA((8,))]
    for _ in range(2):
        shapes += [pltpu.VMEM((TILES, 128, 128), F32)] * len(MODULE_FIELDS)
        shapes += [pltpu.VMEM((128, CELLS), BF16)] * len(FLAT_FIELDS)
        shapes += [
            pltpu.VMEM((512, CELLS), BF16),
            pltpu.VMEM((TILES, 8, 128), F32),
            pltpu.VMEM((TILES, 8, 128), F32),
            pltpu.VMEM((512, 128), BF16),
            pltpu.VMEM((128, 128), BF16),
            pltpu.VMEM((128, 128), BF16),
            pltpu.VMEM((WIDE, WIDE), BF16),
            pltpu.VMEM((WIDE, WIDE), BF16),
        ]
    shapes += [pltpu.VMEM((TILES, 128, 128), F32)] * 4
    shapes += [
        pltpu.VMEM((DEVICES * SGL, 128), F32),
        pltpu.VMEM((WIDE, WIDE), BF16),
        pltpu.VMEM((12, DEVICES, 3, 4, 128), BF16),
        pltpu.VMEM((12, DEVICES, 3, 4, 128), BF16),
        pltpu.VMEM((TILES, 128, 128), F32),
        pltpu.VMEM((DEVICES * GRD, 128), F32),
    ]
    shapes += [pltpu.VMEM((DEVICES, GRD, 128), BF16)] * 3
    shapes += [pltpu.VMEM((DEVICES, TAIL, 128), BF16)] * 3
    shapes += [
        pltpu.SemaphoreType.DMA((16,)),
        pltpu.SemaphoreType.DMA((16,)),
        pltpu.SemaphoreType.DMA((8,)),
    ]
    return shapes + [pltpu.VMEM(v.shape, F32) for v in results]


def publish(*refs):
    src, dst, held, sem_in, sem_out = refs[:8], refs[8:16], refs[16:24], refs[24], refs[25]
    ins = [pltpu.make_async_copy(src[j], held[j], sem_in.at[j]) for j in range(8)]
    outs = [pltpu.make_async_copy(held[j], dst[j], sem_out.at[j]) for j in range(8)]
    for copy in ins:
        copy.start()
    for copy_in, copy_out in zip(ins, outs):
        copy_in.wait()
        copy_out.start()
    for copy in outs:
        copy.wait()


def local(*args):
    anywhere = pl.BlockSpec(memory_space=pl.ANY)
    pair = jax.ShapeDtypeStruct((BI, BK, C), F32)
    square = jax.ShapeDtypeStruct((C, C), F32)
    proj = jax.ShapeDtypeStruct((C, 4 * C), F32)
    shapes = (pair, pair, proj, square, square, proj, square, square)
    results = pl.pallas_call(
        kernel,
        out_shape=shapes,
        in_specs=[anywhere] * 8,
        out_specs=(anywhere,) * 8,
        scratch_shapes=scratch(args, shapes),
        compiler_params=pltpu.CompilerParams(
            has_side_effects=True, collective_id=0, vmem_limit_bytes=58 * 2**20
        ),
        name="triangles",
    )(*args)
    return pl.pallas_call(
        publish,
        out_shape=shapes,
        in_specs=[anywhere] * 8,
        out_specs=(anywhere,) * 8,
        scratch_shapes=[pltpu.VMEM(v.shape, F32) for v in shapes] + [pltpu.SemaphoreType.DMA((8,))] * 2,
        name="publish",
    )(*results)


def solution(mesh):
    specs = (P("row", "col", None), P("row", "col", None), P(), P(), P(), P(), P(), P())
    return jax.shard_map(local, mesh=mesh, in_specs=specs, out_specs=specs, check_vma=False)
```

```python
import types

import jax
import jax.numpy as jnp
from jax import lax
from jax.experimental import pallas as pl
from jax.experimental.pallas import tpu as pltpu
from jax.sharding import PartitionSpec as P

F32 = jnp.float32
BF16 = jnp.bfloat16
EPSILON = 1e-05
MESH = pl.DeviceIdType.MESH

ROWS, COLS, DEVICES = 16, 8, 128
BI, BK, C = 24, 48, 128
TILES = 12
SLOT = 64
WIDE = COLS * SLOT
CELLS = TILES * 128
SGL = 16
GRD, TAIL = 8, 4
OFFSETS = sorted(
    ((dx, dy, dz, dc) for dx in range(4) for dy in range(4) for dz in range(4) for dc in range(2)),
    key=lambda o: -sum(min(v, 4 - v) for v in o[:3]),
)
OFFSETS.remove((0, 0, 0, 0))

MODULE_FIELDS = ("n", "s1", "p2", "s3", "p4", "gate", "u", "lifted")
FLAT_FIELDS = ("nb", "ub", "gl", "gg")


def dot(a, b, ca=1, cb=0):
    return lax.dot_general(a, b, (((ca,), (cb,)), ((), ())), preferred_element_type=F32)


def norm(p):
    d = p - jnp.mean(p, axis=0, keepdims=True)
    r = lax.rsqrt(jnp.mean(d * d, axis=0, keepdims=True) + EPSILON)
    return d * r, r


def norm_back(q, n, r):
    return (q - jnp.mean(q, axis=0, keepdims=True) - n * jnp.mean(q * n, axis=0, keepdims=True)) * r


def lanes(t):
    return pl.ds(pl.multiple_of(t * 128, 128), 128)


def kernel(*refs):
    sources, results, taken, isem = refs[:8], refs[8:16], refs[16:24], refs[24]
    pair, cot, wp_o, wg_o, wl_o, wp_i, wg_i, wl_i = taken
    it = iter(refs[25:])

    def enter(j):
        return pltpu.make_async_copy(sources[j], taken[j], isem.at[j])

    for j in (0, 2, 3, 4, 5, 6, 7, 1):
        enter(j).start()

    def module(wp, wg, wl):
        m = types.SimpleNamespace(wp=wp, wg=wg, wl=wl)
        for name in MODULE_FIELDS + FLAT_FIELDS + ("gp", "r", "ur", "wpt", "wgt", "wlt", "ml", "mr"):
            setattr(m, name, next(it))
        return m

    out, inc = module(wp_o, wg_o, wl_o), module(wp_i, wg_i, wl_i)
    xt, ct, mt, gt, stage, gmat, snd, rec, pg = (next(it) for _ in range(9))
    ws, ga, gb, ssem, rsem = next(it), (next(it), next(it), next(it)), (next(it), next(it), next(it)), next(it), next(it)
    osem = next(it)
    held = tuple(it)
    res, grad, dpo, dgo, dlo, dpi, dgi, dli = held

    row, col = lax.axis_index("row"), lax.axis_index("col")
    me = row * COLS + col
    x = row // 8 * 2 + lax.rem(col, 2)
    xs = [lax.rem(x + d, 4) for d in range(4)]
    row_x = [v // 2 * 8 for v in xs]
    col_x = [lax.rem(v, 2) for v in xs]
    row_z = [lax.rem(lax.rem(row, 8) // 2 + d, 4) * 2 for d in range(4)]
    col_y = [lax.rem(col // 2 + d, 4) * 2 for d in range(4)]
    row_c = [lax.rem(row + d, 2) for d in range(2)]

    def peers(visit):
        for dx, dy, dz, dc in OFFSETS:
            visit(row_x[dx] + row_z[dz] + row_c[dc], col_y[dy] + col_x[dx])

    barrier = pltpu.get_barrier_semaphore()
    peers(lambda rr, cc: pl.semaphore_signal(barrier, inc=1, device_id=(rr, cc), device_id_type=MESH))

    def start(src, dst, k, rr, cc):
        pltpu.make_async_remote_copy(
            src, dst, ssem.at[k], rsem.at[k], device_id=(rr, cc), device_id_type=MESH
        ).start()

    def drain(ref, sem, k):
        span = ref.at[pl.ds(0, DEVICES - 1)]
        pltpu.make_async_copy(span, span, sem.at[k]).wait()

    def leave(j):
        return pltpu.make_async_copy(held[j], results[j], osem.at[j])

    def arrive(ref, k):
        drain(ref, rsem, k)

    def piece(p):
        return stage[pl.ds(pl.multiple_of(p * SGL, SGL), SGL), :]

    def put(ref, p, value):
        for j in range(3):
            ref[p, j] = value[4 * j : 4 * j + 4].astype(BF16)

    def send_staged(k):
        def visit(rr, cc):
            p = rr * COLS + cc
            put(snd.at[k], p, piece(p))
            start(snd.at[k, p], rec.at[k, me], k, rr, cc)

        peers(visit)
        put(rec.at[k], me, piece(me))

    def send_ready(src, dst, k):
        peers(lambda rr, cc: start(src.at[rr * COLS + cc], dst.at[me], k, rr, cc))
        dst[me] = src[me]

    def unpack(k):
        def step(a, carry):
            for b in range(COLS):
                p = a * COLS + b
                for j in range(3):
                    stage[pl.ds(pl.multiple_of(p * SGL, SGL) + 4 * j, 4), :] = rec[k, p, j].astype(F32)
            return carry

        lax.fori_loop(0, ROWS, step, 0, unroll=2)

    def tiles(body):
        lax.fori_loop(0, TILES, lambda t, carry: (body(t), carry)[1], 0, unroll=6)

    low = lax.broadcasted_iota(jnp.int32, (BI, 128), 1) < SLOT
    top = lax.broadcasted_iota(jnp.int32, (BI, 128), 0) < TILES
    gap8 = jnp.zeros((8, 128), F32)
    gap16 = jnp.zeros((16, 128), F32)

    def swap_lanes(a):
        return pltpu.roll(a, SLOT, 1)

    def swap_rows(a):
        return pltpu.roll(a, TILES, 0)

    def halves(a, b):
        return jnp.where(low, a, swap_lanes(b)), jnp.where(low, swap_lanes(a), b)

    def assemble(k, whole):
        unpack(k)

        def step(r2, carry):
            at = pl.ds(pl.multiple_of(r2 * SLOT, SLOT), SLOT)
            for m in range(COLS // 2):
                ls = []
                for s in range(2):
                    p = (2 * r2 + s) * COLS + 2 * m
                    a, b = (jnp.concatenate([piece(q), gap8], axis=0) for q in (p, p + 1))
                    o0, o1 = halves(a, b)
                    ls.append(jnp.where(top, o0, swap_rows(o1)))
                whole[at, m * 128 : (m + 1) * 128] = jnp.concatenate(ls + [gap16], axis=0).astype(BF16)
            return carry

        lax.fori_loop(0, ROWS // 2, step, 0, unroll=2)

    half = row // 4

    def send_rows(rows_of, k):
        def step(i, carry):
            q = lax.rem(half // 2 + 1 + i // 2, 2) * 2 + lax.rem(half + 1 + i, 2)
            block = rows_of(pl.ds(pl.multiple_of(q * 128, 128), 128))
            for s4 in range(4):
                lo = SLOT * (s4 // 2) + BI * (s4 % 2)
                for m in range(COLS // 2):
                    p = (4 * q + s4) * COLS + 2 * m
                    first = block[lo : lo + BI, m * 128 : (m + 1) * 128]
                    a, b = halves(first, swap_rows(first))
                    put(snd.at[k], p, a)
                    put(snd.at[k], p + 1, b)
            for d in (2, 1, 3, 0):
                for s4 in range(4):
                    for x_lo in range(2):
                        rr, cc = 4 * q + s4, col_y[d] + x_lo
                        p = rr * COLS + cc
                        if d:
                            start(snd.at[k, p], rec.at[k, me], k, rr, cc)
                        else:
                            @pl.when(p != me)
                            def _():
                                start(snd.at[k, p], rec.at[k, me], k, rr, cc)
            return carry

        lax.fori_loop(0, WIDE // 128, step, 0)
        rec[k, me] = snd[k, me]

    def into_tiles(src, dst):
        def body(t):
            rows = jnp.concatenate([src[t], gap16, src[TILES + t], gap16], axis=0)
            dst[t] = rows.T

        tiles(body)

    def out_tile(t, value, dst):
        back = value.T
        dst[t] = back[:BK]
        dst[TILES + t] = back[SLOT : SLOT + BK]

    def strided(t):
        return stage[pl.ds(t, 128, stride=SGL), :]

    def put_strided(t, value):
        stage[pl.ds(t, 128, stride=SGL), :] = value

    def project_left(t, x, m):
        n, r = norm(x)
        nb = n.astype(BF16)
        m.n[t] = n
        m.r[t] = jnp.broadcast_to(r, (8, 128))
        m.nb[:, lanes(t)] = nb
        s1 = jax.nn.sigmoid(dot(m.wpt[0:128], nb))
        p2 = dot(m.wpt[128:256], nb)
        m.s1[t] = s1
        m.p2[t] = p2
        put_strided(t, s1 * p2)

    def project_right(t, m):
        nb = m.nb[:, lanes(t)]
        s3 = jax.nn.sigmoid(dot(m.wpt[256:384], nb))
        p4 = dot(m.wpt[384:512], nb)
        m.s3[t] = s3
        m.p4[t] = p4
        put_strided(t, s3 * p4)

    def project_gate(t, m):
        m.gate[t] = jax.nn.sigmoid(dot(m.wgt[...], m.nb[:, lanes(t)]))

    def finish(t, tri, base, m):
        u, r = norm(tri)
        ub = u.astype(BF16)
        m.u[t] = u
        m.ur[t] = jnp.broadcast_to(r, (8, 128))
        m.ub[:, lanes(t)] = ub
        lifted = dot(m.wlt[...], ub)
        m.lifted[t] = lifted
        return base + m.gate[t] * lifted

    def head_back(t, g, m):
        gate = m.gate[t]
        through = g * gate
        gl = through.astype(BF16)
        m.gl[:, lanes(t)] = gl
        m.gg[:, lanes(t)] = (through * m.lifted[t] * (1.0 - gate)).astype(BF16)
        gunit = dot(m.wl[...], gl)
        put_strided(t, norm_back(gunit, m.u[t], m.ur[t][0:1]))

    def pre_back_left(t, m):
        s1 = m.s1[t]
        a = strided(t) * s1
        m.gp[0:128, lanes(t)] = (a * m.p2[t] * (1.0 - s1)).astype(BF16)
        m.gp[128:256, lanes(t)] = a.astype(BF16)
        pg[t] = dot(m.wp[:, 0:256], m.gp[0:256, lanes(t)]) + dot(m.wg[...], m.gg[:, lanes(t)])

    def pre_back_right(t, m):
        s3 = m.s3[t]
        b = strided(t) * s3
        m.gp[256:384, lanes(t)] = (b * m.p4[t] * (1.0 - s3)).astype(BF16)
        m.gp[384:512, lanes(t)] = b.astype(BF16)

    def tail_back(t, g, m):
        gn = pg[t] + dot(m.wp[:, 256:512], m.gp[256:512, lanes(t)])
        return g + norm_back(gn, m.n[t], m.r[t][0:1])

    def rows_of_grads(j, size, value):
        ws[pl.ds(j, 128, stride=size), :] = value

    def proj_grads(m, size, columns):
        for j in columns:
            rows_of_grads(j, size, dot(m.nb[...], m.gp[j * 128 : (j + 1) * 128, :], 1, 1))

    def pack_grads(snd, size):
        def step(a, carry):
            for b in range(COLS):
                at = pl.multiple_of(a * (COLS * size), 8) + b * size
                snd[a * COLS + b] = ws[pl.ds(at, size), :].astype(BF16)
            return carry

        lax.fori_loop(0, ROWS, step, 0, unroll=2)

    def sum_grads(rec, whole, size):
        whole[me] = lax.fori_loop(
            0,
            ROWS,
            lambda a, acc: acc + jnp.sum(rec[pl.ds(a * COLS, COLS)].astype(F32), axis=0),
            jnp.zeros((size, 128), F32),
        ).astype(BF16)

    def spread_grads(whole, k):
        peers(lambda rr, cc: start(whole.at[me], whole.at[me], k, rr, cc))

    def unpack_grads(whole, size):
        def step(a, carry):
            for b in range(COLS):
                at = pl.multiple_of(a * (COLS * size), 8) + b * size
                ws[pl.ds(at, size), :] = whole[a * COLS + b].astype(F32)
            return carry

        lax.fori_loop(0, ROWS, step, 0, unroll=2)

    def write_rows(j, size, dst):
        dst[...] = ws[pl.ds(j, 128, stride=size), :]

    def turn(m, first):
        for j in range(first, first + 3):
            enter(j).wait()
        m.wpt[...] = m.wp[...].T
        m.wgt[...] = m.wg[...].T
        m.wlt[...] = m.wl[...].T

    enter(0).wait()
    into_tiles(pair, xt)
    turn(out, 2)
    tiles(lambda t: project_left(t, xt[t], out))
    pl.semaphore_wait(barrier, DEVICES - 1)
    send_staged(0)
    tiles(lambda t: project_right(t, out))
    send_staged(1)
    tiles(lambda t: project_gate(t, out))
    enter(1).wait()
    into_tiles(cot, ct)
    turn(inc, 5)
    arrive(rec.at[0], 0)
    assemble(0, out.ml)
    arrive(rec.at[1], 1)
    assemble(1, out.mr)
    send_rows(lambda at: dot(out.ml[at, :], out.mr[...], 1, 1), 2)
    arrive(rec.at[2], 2)
    unpack(2)

    def middle_tile(t):
        mid = finish(t, strided(t), xt[t], out)
        mt[t] = mid

    tiles(middle_tile)
    tiles(lambda t: project_left(t, mt[t], inc))
    send_staged(3)
    tiles(lambda t: project_right(t, inc))
    send_staged(4)
    tiles(lambda t: project_gate(t, inc))
    arrive(rec.at[3], 3)
    assemble(3, inc.ml)
    arrive(rec.at[4], 4)
    assemble(4, inc.mr)
    send_rows(lambda at: dot(inc.ml[:, at], inc.mr[...], 0, 0), 5)
    arrive(rec.at[5], 5)
    unpack(5)

    def result_tile(t):
        mt[t] = finish(t, strided(t), mt[t], inc)
        head_back(t, ct[t], inc)

    tiles(result_tile)
    send_staged(6)
    tiles(lambda t: out_tile(t, mt[t], res))
    leave(0).start()
    arrive(rec.at[6], 6)
    assemble(6, gmat)
    send_rows(lambda at: dot(inc.mr[at, :], gmat[...], 1, 1), 7)
    send_rows(lambda at: dot(inc.ml[at, :], gmat[...], 1, 0), 8)
    arrive(rec.at[7], 7)
    unpack(7)
    tiles(lambda t: pre_back_left(t, inc))
    arrive(rec.at[8], 8)
    unpack(8)

    def grad_middle_tile(t):
        gt[t] = tail_back(t, ct[t], inc)

    tiles(lambda t: pre_back_right(t, inc))
    tiles(grad_middle_tile)
    tiles(lambda t: head_back(t, gt[t], out))
    send_staged(9)
    proj_grads(inc, GRD, range(4))
    rows_of_grads(4, GRD, dot(inc.nb[...], inc.gg[...], 1, 1))
    rows_of_grads(5, GRD, dot(inc.ub[...], inc.gl[...], 1, 1))
    rows_of_grads(6, GRD, dot(out.nb[...], out.gg[...], 1, 1))
    rows_of_grads(7, GRD, dot(out.ub[...], out.gl[...], 1, 1))
    pack_grads(ga[0], GRD)
    arrive(rec.at[9], 9)
    assemble(9, gmat)
    send_rows(lambda at: dot(gmat[at, :], out.mr[...], 1, 0), 10)
    send_rows(lambda at: dot(gmat[:, at], out.ml[...], 0, 0), 11)
    send_ready(ga[0], ga[1], 12)
    arrive(rec.at[10], 10)
    unpack(10)
    tiles(lambda t: pre_back_left(t, out))
    proj_grads(out, TAIL, (0, 1))
    arrive(rec.at[11], 11)
    unpack(11)
    tiles(lambda t: pre_back_right(t, out))
    proj_grads(out, TAIL, (2, 3))
    pack_grads(gb[0], TAIL)
    send_ready(gb[0], gb[1], 14)
    arrive(ga[1], 12)
    sum_grads(ga[1], ga[2], GRD)
    spread_grads(ga[2], 13)
    tiles(lambda t: out_tile(t, tail_back(t, gt[t], out), grad))
    leave(1).start()
    arrive(gb[1], 14)
    sum_grads(gb[1], gb[2], TAIL)
    spread_grads(gb[2], 15)
    arrive(ga[2], 13)
    unpack_grads(ga[2], GRD)
    for j in range(4):
        write_rows(j, GRD, dpi.at[:, j * 128 : (j + 1) * 128])
    for j, dst in ((4, dgi), (5, dli), (6, dgo), (7, dlo)):
        write_rows(j, GRD, dst)
    for j in range(3, 8):
        leave(j).start()
    arrive(gb[2], 15)
    unpack_grads(gb[2], TAIL)
    for j in range(4):
        write_rows(j, TAIL, dpo.at[:, j * 128 : (j + 1) * 128])
    leave(2).start()

    for k in range(12):
        drain(snd.at[k], ssem, k)
    for g, k in ((ga, 12), (gb, 14)):
        drain(g[0], ssem, k)
        drain(g[2], ssem, k + 1)
    for j in range(8):
        leave(j).wait()


def scratch(arguments, results):
    shapes = [pltpu.VMEM(v.shape, v.dtype) for v in arguments] + [pltpu.SemaphoreType.DMA((8,))]
    for _ in range(2):
        shapes += [pltpu.VMEM((TILES, 128, 128), F32)] * len(MODULE_FIELDS)
        shapes += [pltpu.VMEM((128, CELLS), BF16)] * len(FLAT_FIELDS)
        shapes += [
            pltpu.VMEM((512, CELLS), BF16),
            pltpu.VMEM((TILES, 8, 128), F32),
            pltpu.VMEM((TILES, 8, 128), F32),
            pltpu.VMEM((512, 128), BF16),
            pltpu.VMEM((128, 128), BF16),
            pltpu.VMEM((128, 128), BF16),
            pltpu.VMEM((WIDE, WIDE), BF16),
            pltpu.VMEM((WIDE, WIDE), BF16),
        ]
    shapes += [pltpu.VMEM((TILES, 128, 128), F32)] * 4
    shapes += [
        pltpu.VMEM((DEVICES * SGL, 128), F32),
        pltpu.VMEM((WIDE, WIDE), BF16),
        pltpu.VMEM((12, DEVICES, 3, 4, 128), BF16),
        pltpu.VMEM((12, DEVICES, 3, 4, 128), BF16),
        pltpu.VMEM((TILES, 128, 128), F32),
        pltpu.VMEM((DEVICES * GRD, 128), F32),
    ]
    shapes += [pltpu.VMEM((DEVICES, GRD, 128), BF16)] * 3
    shapes += [pltpu.VMEM((DEVICES, TAIL, 128), BF16)] * 3
    shapes += [
        pltpu.SemaphoreType.DMA((16,)),
        pltpu.SemaphoreType.DMA((16,)),
        pltpu.SemaphoreType.DMA((8,)),
    ]
    return shapes + [pltpu.VMEM(v.shape, F32) for v in results]


def publish(*refs):
    src, dst, held, sem_in, sem_out = refs[:8], refs[8:16], refs[16:24], refs[24], refs[25]
    ins = [pltpu.make_async_copy(src[j], held[j], sem_in.at[j]) for j in range(8)]
    outs = [pltpu.make_async_copy(held[j], dst[j], sem_out.at[j]) for j in range(8)]
    for copy in ins:
        copy.start()
    for copy_in, copy_out in zip(ins, outs):
        copy_in.wait()
        copy_out.start()
    for copy in outs:
        copy.wait()


def local(*args):
    anywhere = pl.BlockSpec(memory_space=pl.ANY)
    pair = jax.ShapeDtypeStruct((BI, BK, C), F32)
    square = jax.ShapeDtypeStruct((C, C), F32)
    proj = jax.ShapeDtypeStruct((C, 4 * C), F32)
    shapes = (pair, pair, proj, square, square, proj, square, square)
    results = pl.pallas_call(
        kernel,
        out_shape=shapes,
        in_specs=[anywhere] * 8,
        out_specs=(anywhere,) * 8,
        scratch_shapes=scratch(args, shapes),
        compiler_params=pltpu.CompilerParams(
            has_side_effects=True, collective_id=0, vmem_limit_bytes=58 * 2**20
        ),
        name="triangles",
    )(*args)
    return pl.pallas_call(
        publish,
        out_shape=shapes,
        in_specs=[anywhere] * 8,
        out_specs=(anywhere,) * 8,
        scratch_shapes=[pltpu.VMEM(v.shape, F32) for v in shapes] + [pltpu.SemaphoreType.DMA((8,))] * 2,
        name="publish",
    )(*results)


def solution(mesh):
    specs = (P("row", "col", None), P("row", "col", None), P(), P(), P(), P(), P(), P())
    return jax.shard_map(local, mesh=mesh, in_specs=specs, out_specs=specs, check_vma=False)
```
